256 devices in a mesh: visit: 32 (over x, z), sky: 8 (over y, core).
Axes of the slice: x: 4, y: 4, z: 8, core: 2. Of those that a mesh axis runs over, the one named last changes fastest.
Arguments:
- ccd_tiles: bfloat16 [256, 64, 2048], P(('visit', 'sky')), may hold values from -6 to 6
- row_taps: bfloat16 [5, 41], replicated, may hold values from -1 to 1
- col_taps: bfloat16 [5, 41], replicated, may hold values from -1 to 1
- psf_coeffs: float32 [256, 5, 3], P(('visit', 'sky')), may hold values from -3 to 3
- warp_start_x: int32 [256, 2048], P(('visit', 'sky')), may hold values from 2 to 2044
- warp_frac_x: float32 [256, 2048], P(('visit', 'sky')), may hold values from 0.05 to 0.95
- warp_start_y: int32 [256, 64], P(('visit', 'sky')), may hold values from 2 to 60
- warp_frac_y: float32 [256, 64], P(('visit', 'sky')), may hold values from 0.05 to 0.95
- tile_weight: bfloat16 [256], P(('visit', 'sky')), may hold values from 0.25 to 4
- strip_owner: int32 [256, 16, 1], P(('visit', 'sky')), may hold values from 0 to 31; in each aligned block of 16 rows (0 to 15, 16 to 31, ..., all dimensions but the last counted through in order) at most 2 rows name the same one
- strip_block: int32 [256, 16], P(('visit', 'sky')), may hold values from 0 to 15
Outputs:
- coadd: float32 [512, 65536], P('sky', 'visit')
- detection: float32 [512, 65536], P('sky', 'visit')
The draws below stay inside these ranges and needn't reach their ends.
Inputs may be any that keep to these rules, and one draw needn't show every extreme that they name: `strip_owner`: among the strips of one device (aligned blocks of 16 strips) no patch is named more than 2 times; some patch is named exactly 2 times in some device's strips.
All inputs are finite; a program needn't handle non-finite values.
Results may differ from the reference program's by a relative error of at most 0.0068.
Values may be sent and summed in bfloat16 or wider, within the bound.
No kernel may reach another device: no remote copies, remote signals or barrier semaphores. Data moves between devices by JAX's collectives and lax.ppermute only.
A program may use at most 128 MiB of HBM per device.

```python
import math
import jax
import jax.numpy as jnp
import numpy as np
from jax import lax

W = 2048
R = 64
TILES_DEV = 1
NB = 5
KW = 41
HALO = 20
SPT = 16
CAP = 2
TILES = 256
NR = 512
NC = 65536
N_VISIT = 32
N_SKY = 8


def draw_warp_start_x(key, part):
    key = jax.random.fold_in(key, 11)
    key_shift, key_jitter = jax.random.split(key)
    shift_val = jax.random.randint(key_shift, (TILES, 1), -2, 3)
    jitter_val = jax.random.randint(key_jitter, (TILES, W), -1, 2)
    return jnp.clip(jnp.arange(W)[None, :] + shift_val + jitter_val, 2, W - 4).astype(jnp.int32)


def draw_warp_start_y(key, part):
    key = jax.random.fold_in(key, 12)
    key_shift, key_jitter = jax.random.split(key)
    shift_val = jax.random.randint(key_shift, (TILES, 1), -2, 3)
    jitter_val = jax.random.randint(key_jitter, (TILES, R), -1, 2)
    return jnp.clip(jnp.arange(R)[None, :] + shift_val + jitter_val, 2, R - 4).astype(jnp.int32)


def place_ends(array, key, least, top_value):
    longest = array.shape.index(max(array.shape))
    spots = []
    for shift in (0, 1):
        where = [jax.random.randint(jax.random.fold_in(key, axis), (), 0, length) for axis, length in enumerate(array.shape)]
        where[longest] = (where[longest] + shift) % array.shape[longest]
        spots.append(tuple(where))
    return array.at[spots[0]].set(least).at[spots[1]].set(top_value)


def block_levels(key, dims, cuts, low, top_value):
    loudness, own = 1.0, jax.random.fold_in(key, 6)
    for axis_at, parts in cuts:
        heights = jnp.exp(jax.random.uniform(jax.random.fold_in(own, axis_at), (parts,), jnp.float32, low / len(cuts), top_value / len(cuts)))
        loudness = loudness * jnp.repeat(heights, dims[axis_at] // parts).reshape([-1 if axis == axis_at else 1 for axis in range(len(dims))])
    return loudness


def routed_block(rng, own, number, rows, amount, top, reach, skew):
    sequence = jax.random.permutation(rng, amount)
    packed, ordinary = portions_of(amount, rows * top, reach, skew, True), portions_of(amount, rows * top, reach, skew, False)
    places = jnp.arange(amount)

    def named(lengths, rotation):
        used = int((lengths > 0).sum())
        fixed = max(1, used // 4)
        moved = fixed + (places - fixed + rotation * (used - fixed)) % max(1, amount - fixed)
        return jnp.zeros((amount,), jnp.int32).at[sequence[jnp.where(places < fixed, places, moved)]].set(jnp.asarray(lengths, jnp.int32))

    lengths = jnp.where(number % 4 == 0, named(packed, number // 4), named(ordinary, number - number // 4 - 1))
    mixed = jax.random.permutation(jax.random.fold_in(own, 3), amount)
    giver, taker = mixed[0:amount // 2 * 2:2], mixed[1:amount // 2 * 2:2]
    room = jnp.minimum(lengths[giver] - 1, reach - lengths[taker]) // 2
    room = jnp.where((giver == sequence[0]) | (taker == sequence[0]) | (lengths[taker] == 0), 0, jnp.maximum(room, 0))
    moved = jax.random.randint(jax.random.fold_in(own, 4), (amount // 2,), 0, 1 << 20) % (room + 1)
    lengths = lengths.at[giver].add(-moved).at[taker].add(moved)
    items = jnp.searchsorted(jnp.cumsum(lengths), jnp.arange(rows * top), side="right").astype(jnp.int32)
    listing = items.reshape(top, rows).T
    listing = listing[jax.random.permutation(jax.random.fold_in(own, 1), rows)]
    rotation = jax.random.randint(jax.random.fold_in(own, 2), (rows, 1), 0, top)
    return jnp.take_along_axis(listing, (jnp.arange(top)[None, :] + rotation) % top, axis=1)


def portions_of(count, total, most, slope, full):
    portions = [(1 << 20) // math.isqrt(standing ** slope) + 1 for standing in range(1, count + 1)]
    largest = most if full else min(most, max(-(-total // count), total * portions[0] // sum(portions)))
    least = 1 if total - largest >= count - 1 else 0
    holding, rest = [largest] + [least] * (count - 1), total - largest - least * (count - 1)
    while rest > 0:
        movable = [i for i in range(1, count) if holding[i] < largest] or [i for i in range(1, count) if holding[i] < most]
        mass, budget = sum([portions[i] for i in movable]), rest
        for i in movable:
            more = min(most - holding[i], max(1, budget * portions[i] // mass), rest)
            holding[i] = holding[i] + more
            rest = rest - more
    return np.array(holding)


def centred(key, extent, width, most, pieces=(), kind=jnp.bfloat16):
    values = width * jax.random.normal(key, extent, jnp.float32)
    if pieces:
        values = values * block_levels(key, extent, pieces, -0.22, 0.18)
    return jnp.clip(values, -most, most).astype(kind)


def setup_inputs(seed: int = 0) -> dict:
    key_of = jax.random.split(jax.random.key(seed), 12)
    ccd_tiles = centred(key_of[0], (TILES, R, W), 1.0, 6.0, ((0, 256),))
    row_taps = centred(key_of[1], (NB, KW), KW ** -0.5, 1.0)
    col_taps = centred(key_of[2], (NB, KW), KW ** -0.5, 1.0)
    psf_coeffs = centred(key_of[3], (TILES, NB, 3), 0.5, 3.0, ((0, 256),), jnp.float32)
    warp_start_x = draw_warp_start_x(jax.random.fold_in(key_of[11], 71), 0)
    warp_frac_x = jnp.clip(0.05 + 0.9 * jax.random.uniform(key_of[5], (TILES, W), jnp.float32) ** block_levels(key_of[5], (TILES, W), ((0, 256),), -0.2, 0.2), 0.05, 0.95)
    warp_start_y = draw_warp_start_y(jax.random.fold_in(key_of[11], 71), 0)
    warp_frac_y = jnp.clip(0.05 + 0.9 * jax.random.uniform(key_of[7], (TILES, R), jnp.float32) ** block_levels(key_of[7], (TILES, R), ((0, 256),), -0.2, 0.2), 0.05, 0.95)
    tile_weight = jnp.clip(jnp.exp(math.log(4.0) - 2.7725887 * jax.random.uniform(key_of[8], (TILES,), jnp.float32) ** block_levels(key_of[8], (TILES,), ((0, 256),), -0.2, 0.2)), 0.25, 4.0).astype(jnp.bfloat16)
    strip_owner_keys = jax.random.split(jax.random.fold_in(key_of[9], 1), TILES * SPT // (TILES_DEV * SPT))
    strip_owner_turns = jax.random.permutation(jax.random.fold_in(key_of[9], 3), TILES * SPT // (TILES_DEV * SPT))
    strip_owner = jax.vmap(lambda own, number: routed_block(jax.random.fold_in(key_of[9], 2), own, number, TILES_DEV * SPT, N_VISIT, 1, CAP, 2))(strip_owner_keys, strip_owner_turns).reshape((TILES, SPT, 1))
    strip_block = place_ends(jax.random.randint(key_of[10], (TILES, SPT), 0, SPT), jax.random.fold_in(key_of[10], 1), 0, SPT - 1).astype(jnp.int32)
    return {"ccd_tiles": ccd_tiles, "row_taps": row_taps, "col_taps": col_taps, "psf_coeffs": psf_coeffs, "warp_start_x": warp_start_x, "warp_frac_x": warp_frac_x, "warp_start_y": warp_start_y, "warp_frac_y": warp_frac_y, "tile_weight": tile_weight, "strip_owner": strip_owner, "strip_block": strip_block}


def lanczos(offset):
    return 3.0 * jnp.sin(jnp.pi * offset) * jnp.sin(jnp.pi * offset / 3.0) / (jnp.pi * jnp.pi * offset * offset)


def round_half(values):
    return lax.optimization_barrier(values.astype(jnp.bfloat16)).astype(jnp.float32)


def coefficient_maps(coefficients, num_rows, num_cols):
    x_coord = (2.0 * jnp.arange(num_cols, dtype=jnp.float32) - (num_cols - 1)) / (num_cols - 1)
    y_coord = (2.0 * jnp.arange(num_rows, dtype=jnp.float32) - (num_rows - 1)) / (num_rows - 1)
    return (coefficients[:, 0, None, None] + coefficients[:, 1, None, None] * x_coord[None, None, :]
            + coefficients[:, 2, None, None] * y_coord[None, :, None])


def shift_columns(image, tap_values):
    padded = jnp.pad(image, ((0, 0), (HALO, HALO)))
    result = jnp.zeros(image.shape, jnp.float32)
    for offset in range(KW):
        result = result + tap_values[offset].astype(jnp.float32) * padded[:, offset:offset + image.shape[1]]
    return result


def shift_rows(image, tap_values):
    padded = jnp.pad(image, ((HALO, HALO), (0, 0)))
    result = jnp.zeros(image.shape, jnp.float32)
    for offset in range(KW):
        result = result + tap_values[offset].astype(jnp.float32) * padded[offset:offset + image.shape[0], :]
    return result


def lanczos_weights(fractions):
    shifts = jnp.arange(-2, 4).astype(jnp.float32)
    return round_half(lanczos(fractions[:, None] - shifts[None, :]))


def one_tile(row_taps, col_taps, inputs):
    image, coefficients, start_x, frac_x, start_y, frac_y = inputs
    maps = coefficient_maps(coefficients, R, W)
    image_f = image.astype(jnp.float32)
    matched = jnp.zeros((R, W), jnp.float32)
    for basis_idx in range(NB):
        across = round_half(shift_columns(image_f, row_taps[basis_idx]))
        basis_term = shift_rows(across, col_taps[basis_idx])
        matched = matched + maps[basis_idx] * basis_term
    matched = round_half(matched)
    weights_x = lanczos_weights(frac_x)
    col_warped = jnp.zeros((R, W), jnp.float32)
    for shift_idx in range(6):
        taken = jnp.take(matched, (start_x + shift_idx - 2).astype(jnp.int32), axis=1)
        col_warped = col_warped + weights_x[:, shift_idx][None, :] * taken
    col_warped = round_half(col_warped)
    weights_y = lanczos_weights(frac_y)
    warped = jnp.zeros((R, W), jnp.float32)
    for shift_idx in range(6):
        taken = jnp.take(col_warped, (start_y + shift_idx - 2).astype(jnp.int32), axis=0)
        warped = warped + weights_y[:, shift_idx][:, None] * taken
    return warped.astype(jnp.bfloat16)


def reference(ccd_tiles, row_taps, col_taps, psf_coeffs, warp_start_x, warp_frac_x, warp_start_y, warp_frac_y, tile_weight, strip_owner, strip_block):
    warped = lax.map(lambda inputs: one_tile(row_taps, col_taps, inputs),
                     (ccd_tiles, psf_coeffs, warp_start_x, warp_frac_x, warp_start_y, warp_frac_y))
    strips = warped.reshape(TILES, R, SPT, 128).transpose(0, 2, 1, 3).astype(jnp.float32)
    weight_f = tile_weight.astype(jnp.float32)
    tile_group = ((jnp.arange(TILES) // TILES_DEV) % N_SKY).astype(jnp.int32)
    owner_idx = strip_owner[:, :, 0]
    numer = jnp.zeros((N_SKY, N_VISIT, SPT, R, 128), jnp.float32)
    numer = numer.at[tile_group[:, None], owner_idx, strip_block].add(weight_f[:, None, None, None] * strips)
    denom = jnp.zeros((N_SKY, N_VISIT, SPT), jnp.float32)
    denom = denom.at[tile_group[:, None], owner_idx, strip_block].add(jnp.broadcast_to(weight_f[:, None], (TILES, SPT)))
    patches = numer / (denom[:, :, :, None, None] + 1.0)
    coadd = patches.transpose(0, 3, 1, 2, 4).reshape(NR, NC)
    smooth_taps = 1.0 - (jnp.arange(-HALO, HALO + 1).astype(jnp.float32) / 21.0) ** 2
    noise_norm = jnp.sum(smooth_taps * smooth_taps)
    padded = jnp.pad(coadd, ((HALO, HALO), (HALO, HALO)))
    vertical = jnp.zeros((NR, NC + 2 * HALO), jnp.float32)
    for offset in range(2 * HALO + 1):
        vertical = vertical + smooth_taps[offset] * padded[offset:offset + NR, :]
    smoothed = jnp.zeros((NR, NC), jnp.float32)
    for offset in range(2 * HALO + 1):
        smoothed = smoothed + smooth_taps[offset] * vertical[:, offset:offset + NC]
    return coadd, smoothed / noise_norm
```

```python
import jax
import jax.numpy as jnp
from jax import lax
from jax.experimental import pallas as pl
from jax.experimental.pallas import tpu as pltpu
from jax.sharding import PartitionSpec as P

R = 64
W = 2048
NB = 5
KW = 41
HALO = 20
SPT = 16
SLOTS = 2
LANES = 128
META = 16
MSG = SLOTS * R + META
NT = (((1,), (1,)), ((), ()))
TN = (((0,), (0,)), ((), ()))
BF = jnp.bfloat16
F32 = jnp.float32


def dot(left, right, dims=(((1,), (0,)), ((), ())), precision=None):
    return lax.dot_general(left, right, dims, preferred_element_type=F32, precision=precision)


def toeplitz(row, rows, shift=LANES - HALO):
    row = pltpu.roll(row, shift % 8, 1) if shift % 8 else row
    return pltpu.roll(jnp.broadcast_to(row, (rows, row.shape[1])), shift // 8 * 8, 1, stride=1, stride_axis=0)


def lanczos(offset):
    return (
        3.0
        * jnp.sin(jnp.pi * offset)
        * jnp.sin(jnp.pi * offset / 3.0)
        / (jnp.pi * jnp.pi * offset * offset)
    )


def lanczos_weights(frac):
    shape = (8, frac.shape[1])
    shift = lax.broadcasted_iota(jnp.int32, shape, 0) - 2
    return lanczos(jnp.broadcast_to(frac, shape) - shift.astype(F32)).astype(BF).astype(F32)


def tile_kernel(
    coeff_ref, weight_ref, owner_ref, block_ref,
    tile_ref, row_taps_ref, col_taps_ref, start_x_ref, frac_x_ref, start_y_ref, frac_y_ref,
    out_ref,
    taps_ref, stack_ref, matched_ref, shifted_ref, col_ref, count_ref,
):
    taps_ref[...] = jnp.zeros_like(taps_ref)
    taps_ref[0:NB, 0:KW] = row_taps_ref[...].astype(F32)
    taps_ref[8:8 + NB, 0:KW] = col_taps_ref[...].astype(F32)
    row_band = jnp.concatenate([toeplitz(taps_ref[k:k + 1, :], LANES) for k in range(NB)], axis=0).astype(BF)
    col_bands = [toeplitz(taps_ref[8 + k:9 + k, 0:LANES], R)[:, 0:R].astype(BF) for k in range(NB)]
    stack_ref[0:R, :] = jnp.zeros((R, LANES), BF)
    stack_ref[(SPT + 1) * R:(SPT + 2) * R, :] = jnp.zeros((R, LANES), BF)
    for s in range(SPT):
        stack_ref[(s + 1) * R:(s + 2) * R, :] = tile_ref[0, :, s * LANES:(s + 1) * LANES]
    group = 4
    width = group * LANES
    for g in range(SPT // group):
        first = g * group * R
        rows = group * R
        window = jnp.concatenate(
            [stack_ref[first + j * R:first + j * R + rows, :] for j in range(3)], axis=1
        )
        across = dot(window, row_band, NT).astype(BF)
        column = lax.broadcasted_iota(jnp.int32, (1, width), 1) + g * width
        x_coord = (2 * column - (W - 1)).astype(F32) / (W - 1)
        row = lax.broadcasted_iota(jnp.int32, (R, 1), 0)
        y_coord = (2 * row - (R - 1)).astype(F32) / (R - 1)
        matched = jnp.zeros((R, width), F32)
        for k in range(NB):
            term = jnp.concatenate(
                [across[j * R:(j + 1) * R, k * LANES:(k + 1) * LANES] for j in range(group)], axis=1
            )
            basis_term = dot(col_bands[k], term)
            coeff_map = coeff_ref[0, k, 0] + coeff_ref[0, k, 1] * x_coord + coeff_ref[0, k, 2] * y_coord
            matched = matched + coeff_map * basis_term
        matched_ref[:, g * width:(g + 1) * width] = matched.astype(BF).astype(F32)
    for s in range(6):
        shift = (2 - s) % W
        value = matched_ref[...]
        shifted_ref[s * R:(s + 1) * R, :] = (value if shift == 0 else pltpu.roll(value, shift, 1)).astype(BF)
    weights_x = lanczos_weights(frac_x_ref[...])
    chunk = 256
    for c in range(W // chunk):
        cols = slice(c * chunk, (c + 1) * chunk)
        source = lax.broadcasted_iota(jnp.int32, (W, chunk), 0)
        chosen = (source == start_x_ref[:, cols]).astype(F32).astype(BF)
        taken = dot(shifted_ref[...], chosen)
        total = weights_x[0:1, cols] * taken[0:R]
        for s in range(1, 6):
            total = total + weights_x[s:s + 1, cols] * taken[s * R:(s + 1) * R]
        col_ref[:, cols] = total.astype(BF)
    weights_y = lanczos_weights(frac_y_ref[...])
    step = lax.broadcasted_iota(jnp.int32, (R, R), 0) - start_y_ref[...]
    warp_y = jnp.zeros((R, R), F32)
    for s in range(6):
        warp_y = jnp.where(step == s - 2, weights_y[s:s + 1, :], warp_y)
    warped = dot(warp_y.T.astype(BF), col_ref[...]).astype(BF)
    out_ref[...] = jnp.zeros_like(out_ref)
    for o in range(out_ref.shape[0]):
        count_ref[o] = 0
    weight = weight_ref[...].astype(F32)
    row = lax.broadcasted_iota(jnp.int32, (META, LANES), 0)
    slot_of = lax.broadcasted_iota(jnp.int32, (META, LANES), 1) // META
    for s in range(SPT):
        owner = owner_ref[0, s, 0]
        slot = count_ref[owner]
        count_ref[owner] = slot + 1
        out_ref[owner, pl.ds(pl.multiple_of(slot * R, R), R), :] = warped[:, s * LANES:(s + 1) * LANES]
        note = jnp.where(row == 0, weight, jnp.where(row == 1, block_ref[0, s].astype(F32), 0.0))
        note = jnp.where(slot_of == slot, note, 0.0)
        held = out_ref[owner, SLOTS * R:MSG, :].astype(F32)
        out_ref[owner, SLOTS * R:MSG, :] = (held + note).astype(BF)


def sum_kernel(in_ref, coadd_ref):
    peers = in_ref.shape[0]
    depth = peers * SLOTS * META
    notes = []
    per_row = LANES // (SLOTS * META)
    for q in range(peers // per_row):
        total = None
        for j in range(per_row):
            note = in_ref[q * per_row + j, SLOTS * R:MSG, :].astype(F32)
            note = pltpu.roll(note, j * SLOTS * META, 1) if j else note
            total = note if total is None else total + note
        notes.append(total)
    notes = jnp.concatenate(notes, axis=1)
    weight, block = notes[0:1], notes[1:2]
    same = (
        lax.broadcasted_iota(jnp.int32, (META, depth), 0)
        == lax.broadcasted_iota(jnp.int32, (META, depth), 1) % META
    )
    spread = jnp.concatenate(
        [jnp.where(same, jnp.where(block == b, weight, 0.0), 0.0) for b in range(SPT)], axis=0
    ).astype(BF)
    parts = []
    for g in range(R // META):
        pieces = [
            in_ref[v, slot * R + g * META:slot * R + (g + 1) * META, :]
            for v in range(peers) for slot in range(SLOTS)
        ]
        parts.append(jnp.concatenate(pieces, axis=0))
    parts.append(jnp.ones((depth, LANES), BF))
    total = dot(spread, jnp.concatenate(parts, axis=1))
    scale = 1.0 / (total[:, R // META * LANES:] + 1.0)
    for b in range(SPT):
        for g in range(R // META):
            rows = slice(b * META, (b + 1) * META)
            coadd_ref[g * META:(g + 1) * META, b * LANES:(b + 1) * LANES] = (
                total[rows, g * LANES:(g + 1) * LANES] * scale[rows]
            )


def taper_row(width, scale=1.0):
    lane = lax.broadcasted_iota(jnp.int32, (1, width), 1)
    at = (lane - HALO).astype(F32) / 21.0
    return jnp.where(lane < KW, (1.0 - at * at) * scale, 0.0)


def across_kernel(coadd_ref, left_ref, right_ref, out_ref, stack_ref):
    band = toeplitz(taper_row(3 * LANES), LANES)
    stack_ref[0:R, :] = left_ref[...]
    stack_ref[(SPT + 1) * R:(SPT + 2) * R, :] = right_ref[...]
    for s in range(SPT):
        stack_ref[(s + 1) * R:(s + 2) * R, :] = coadd_ref[:, s * LANES:(s + 1) * LANES]
    window = jnp.concatenate([stack_ref[j * R:(j + SPT) * R, :] for j in range(3)], axis=1)
    total = dot(window, band, NT, lax.Precision.HIGHEST)
    for s in range(SPT):
        out_ref[:, s * LANES:(s + 1) * LANES] = total[s * R:(s + 1) * R, :]


EDGE = 24


def down_kernel(mid_ref, above_ref, below_ref, out_ref):
    norm = sum((1.0 - (a / 21.0) ** 2) ** 2 for a in range(-HALO, HALO + 1))
    band = toeplitz(taper_row(LANES, 1.0 / norm), R, EDGE - HALO)
    rows = jnp.concatenate([above_ref[...], mid_ref[...], below_ref[...]], axis=0)
    out_ref[...] = dot(band[:, 0:R + 2 * EDGE], rows, precision=lax.Precision.HIGHEST)


def vmem(n):
    return [pl.BlockSpec(memory_space=pltpu.VMEM)] * n


def smem(n):
    return [pl.BlockSpec(memory_space=pltpu.SMEM)] * n


PARAMS = pltpu.CompilerParams(vmem_limit_bytes=40 * 1024 * 1024)


def neighbours(axis):
    size = lax.axis_size(axis)
    up = [(i, i + 1) for i in range(size - 1)]
    return up, [(j, i) for i, j in up]


def local(
    ccd_tiles, row_taps, col_taps, psf_coeffs, warp_start_x, warp_frac_x, warp_start_y, warp_frac_y,
    tile_weight, strip_owner, strip_block,
):
    peers = lax.axis_size("visit")
    messages = pl.pallas_call(
        tile_kernel,
        out_shape=jax.ShapeDtypeStruct((peers, MSG, LANES), BF),
        in_specs=smem(1) + vmem(1) + smem(2) + vmem(7),
        out_specs=pl.BlockSpec(memory_space=pltpu.VMEM),
        scratch_shapes=[
            pltpu.VMEM((16, 3 * LANES), F32),
            pltpu.VMEM(((SPT + 2) * R, LANES), BF),
            pltpu.VMEM((R, W), F32),
            pltpu.VMEM((6 * R, W), BF),
            pltpu.VMEM((R, W), BF),
            pltpu.SMEM((peers,), jnp.int32),
        ],
        compiler_params=PARAMS,
    )(
        psf_coeffs, tile_weight.reshape(1, 1), strip_owner, strip_block,
        ccd_tiles, row_taps, col_taps, warp_start_x, warp_frac_x, warp_start_y, warp_frac_y,
    )
    received = lax.all_to_all(messages, "visit", 0, 0, tiled=True)
    coadd = pl.pallas_call(
        sum_kernel,
        out_shape=jax.ShapeDtypeStruct((R, W), F32),
        in_specs=vmem(1),
        out_specs=pl.BlockSpec(memory_space=pltpu.VMEM),
        compiler_params=PARAMS,
    )(received)
    up, down = neighbours("visit")
    left = lax.ppermute(coadd[:, W - LANES:], "visit", up)
    right = lax.ppermute(coadd[:, :LANES], "visit", down)
    mid = pl.pallas_call(
        across_kernel,
        out_shape=jax.ShapeDtypeStruct((R, W), F32),
        in_specs=vmem(3),
        out_specs=pl.BlockSpec(memory_space=pltpu.VMEM),
        scratch_shapes=[pltpu.VMEM(((SPT + 2) * R, LANES), F32)],
        compiler_params=PARAMS,
    )(coadd, left, right)
    up, down = neighbours("sky")
    above = lax.ppermute(mid[R - EDGE:], "sky", up)
    below = lax.ppermute(mid[:EDGE], "sky", down)
    detection = pl.pallas_call(
        down_kernel,
        out_shape=jax.ShapeDtypeStruct((R, W), F32),
        in_specs=vmem(3),
        out_specs=pl.BlockSpec(memory_space=pltpu.VMEM),
        compiler_params=PARAMS,
    )(mid, above, below)
    return coadd, detection


def solution(mesh):
    tiles = ("visit", "sky")
    in_specs = (
        P(tiles, None, None),
        P(),
        P(),
        P(tiles, None, None),
        P(tiles, None),
        P(tiles, None),
        P(tiles, None),
        P(tiles, None),
        P(tiles),
        P(tiles, None, None),
        P(tiles, None),
    )
    out_specs = (P("sky", "visit"), P("sky", "visit"))
    return jax.shard_map(local, mesh=mesh, in_specs=in_specs, out_specs=out_specs, check_vma=False)
```

```python
import jax
import jax.numpy as jnp
from jax import lax
from jax.experimental import pallas as pl
from jax.experimental.pallas import tpu as pltpu
from jax.sharding import PartitionSpec as P

R = 64
W = 2048
NB = 5
KW = 41
HALO = 20
SPT = 16
SLOTS = 2
LANES = 128
UNIT = 16
NOTE = SLOTS * R
MSG = NOTE + 2 * UNIT
NOTE_LANES = 2 * UNIT
LEFT_AT = (32, 80)
RIGHT_AT = (52, 100)
EDGE = 24
NT = (((1,), (1,)), ((), ()))
BF = jnp.bfloat16
F32 = jnp.float32


def dot(left, right, dims=(((1,), (0,)), ((), ()))):
    return lax.dot_general(left, right, dims, preferred_element_type=F32)


def iota(shape, dim):
    return lax.broadcasted_iota(jnp.int32, shape, dim)


def roll(value, shift):
    width = value.shape[1]
    return pltpu.roll(value, shift % width, 1) if shift % width else value


def toeplitz(row, rows, shift=LANES - HALO):
    row = roll(row, shift % 8)
    return pltpu.roll(jnp.broadcast_to(row, (rows, row.shape[1])), shift // 8 * 8, 1, stride=1, stride_axis=0)


def lanczos(offset):
    return (
        3.0
        * jnp.sin(jnp.pi * offset)
        * jnp.sin(jnp.pi * offset / 3.0)
        / (jnp.pi * jnp.pi * offset * offset)
    )


def lanczos_weights(frac):
    shape = (8, frac.shape[1])
    shift = iota(shape, 0) - 2
    return lanczos(jnp.broadcast_to(frac, shape) - shift.astype(F32)).astype(BF).astype(F32)


def tile_kernel(
    coeff_hbm, weight_hbm, owner_hbm, block_hbm,
    tile_hbm, row_taps_hbm, col_taps_hbm, start_x_hbm, frac_x_hbm, start_y_hbm, frac_y_hbm,
    out_ref,
    coeff_ref, weight_ref, owner_ref, block_ref,
    tile_ref, row_taps_ref, col_taps_ref, start_x_ref, frac_x_ref, start_y_ref, frac_y_ref,
    sems, taps_ref, stack_ref, matched_ref, shifted_ref, col_ref, count_ref,
):
    pairs = [
        (row_taps_hbm, row_taps_ref), (tile_hbm, tile_ref), (col_taps_hbm, col_taps_ref),
        (coeff_hbm, coeff_ref), (frac_x_hbm, frac_x_ref), (start_x_hbm, start_x_ref),
        (start_y_hbm, start_y_ref), (frac_y_hbm, frac_y_ref), (weight_hbm, weight_ref),
        (owner_hbm, owner_ref), (block_hbm, block_ref),
    ]
    copies = [pltpu.make_async_copy(src, dst, sems.at[n]) for n, (src, dst) in enumerate(pairs)]
    for copy in copies:
        copy.start()
    taps_ref[...] = jnp.zeros_like(taps_ref)
    stack_ref[0:R, :] = jnp.zeros((R, LANES), BF)
    stack_ref[(SPT + 1) * R:(SPT + 2) * R, :] = jnp.zeros((R, LANES), BF)
    peers = out_ref.shape[0]
    for o in range(peers):
        count_ref[o] = 0
    out_ref[...] = jnp.zeros_like(out_ref)
    for copy in copies:
        copy.wait()
    taps_ref[0:NB, 0:KW] = row_taps_ref[...].astype(F32)
    taps_ref[8:8 + NB, 0:KW] = col_taps_ref[...].astype(F32)
    row_band = jnp.concatenate([toeplitz(taps_ref[k:k + 1, :], LANES) for k in range(NB)], axis=0).astype(BF)
    col_bands = [toeplitz(taps_ref[8 + k:9 + k, 0:LANES], R)[:, 0:R].astype(BF) for k in range(NB)]
    for s in range(SPT):
        stack_ref[(s + 1) * R:(s + 2) * R, :] = tile_ref[0, :, s * LANES:(s + 1) * LANES]
    group = 4
    width = group * LANES
    for g in range(SPT // group):
        first = g * group * R
        rows = group * R
        window = jnp.concatenate(
            [stack_ref[first + j * R:first + j * R + rows, :] for j in range(3)], axis=1
        )
        across = dot(window, row_band, NT).astype(BF)
        column = iota((1, width), 1) + g * width
        x_coord = (2 * column - (W - 1)).astype(F32) / (W - 1)
        y_coord = (2 * iota((R, 1), 0) - (R - 1)).astype(F32) / (R - 1)
        matched = jnp.zeros((R, width), F32)
        for k in range(NB):
            term = jnp.concatenate(
                [across[j * R:(j + 1) * R, k * LANES:(k + 1) * LANES] for j in range(group)], axis=1
            )
            basis_term = dot(col_bands[k], term)
            coeff_map = coeff_ref[0, 0, k] + coeff_ref[1, 0, k] * x_coord + coeff_ref[2, 0, k] * y_coord
            matched = matched + coeff_map * basis_term
        matched_ref[:, g * width:(g + 1) * width] = matched.astype(BF).astype(F32)
    for s in range(6):
        shifted_ref[s * R:(s + 1) * R, :] = roll(matched_ref[...], 2 - s).astype(BF)
    weights_x = lanczos_weights(frac_x_ref[...])
    chunk = 256
    for c in range(W // chunk):
        cols = slice(c * chunk, (c + 1) * chunk)
        chosen = (iota((W, chunk), 0) == start_x_ref[:, cols]).astype(F32).astype(BF)
        taken = dot(shifted_ref[...], chosen)
        total = weights_x[0:1, cols] * taken[0:R]
        for s in range(1, 6):
            total = total + weights_x[s:s + 1, cols] * taken[s * R:(s + 1) * R]
        col_ref[:, cols] = total.astype(BF)
    weights_y = lanczos_weights(frac_y_ref[...])
    step = iota((R, R), 0) - start_y_ref[...]
    warp_y = jnp.zeros((R, R), F32)
    for s in range(6):
        warp_y = jnp.where(step == s - 2, weights_y[s:s + 1, :], warp_y)
    warped = dot(warp_y.T.astype(BF), col_ref[...]).astype(BF)
    weight = weight_ref[...].astype(F32)
    row = iota((UNIT, LANES), 0)
    lane = iota((UNIT, LANES), 1)
    base = jnp.where((row == 2) & (lane < NOTE_LANES), weight, 0.0).astype(BF)
    for o in range(peers):
        out_ref[o, NOTE:NOTE + UNIT, :] = base

    def add_edges(owner, strip, lanes, at, count_lane):
        strip = strip.astype(F32)
        for t in range(2):
            piece = jnp.where(lane == count_lane, 1.0, 0.0) if t else jnp.zeros((UNIT, LANES), F32)
            for f in range(2):
                part = strip[(2 * t + f) * UNIT:(2 * t + f + 1) * UNIT]
                inside = (lane >= at[f]) & (lane < at[f] + HALO)
                piece = jnp.where(inside, roll(part, at[f] - lanes), piece)
            rows = slice(NOTE + t * UNIT, NOTE + (t + 1) * UNIT)
            out_ref[owner, rows, :] = (out_ref[owner, rows, :].astype(F32) + piece).astype(BF)

    for s in range(SPT):
        owner, block = owner_ref[0, s], block_ref[0, s]
        slot = count_ref[owner]
        count_ref[owner] = slot + 1
        strip = warped[:, s * LANES:(s + 1) * LANES]
        out_ref[owner, pl.ds(pl.multiple_of(slot * R, R), R), :] = strip
        note = jnp.where(row == 0, weight, jnp.where(row == 1, block.astype(F32), 0.0))
        note = jnp.where((lane // UNIT == slot) & (row < 2), note, 0.0)
        held = out_ref[owner, NOTE:NOTE + UNIT, :].astype(F32)
        out_ref[owner, NOTE:NOTE + UNIT, :] = (held + note).astype(BF)
        pl.when((block == SPT - 1) & (owner < peers - 1))(
            lambda: add_edges(owner + 1, strip, LANES - HALO, LEFT_AT, 0)
        )
        pl.when((block == 0) & (owner > 0))(lambda: add_edges(owner - 1, strip, 0, RIGHT_AT, 1))


def split(value):
    high = value.astype(BF)
    return high, (value - high.astype(F32)).astype(BF)


def taper_bands(width, rows, shift):
    lane = iota((1, width), 1)
    at = lane - HALO
    taps = jnp.where(lane < KW, 441 - at * at, 0).astype(F32)
    high, low = split(toeplitz(taps, rows, shift))
    return jnp.concatenate([high, low], axis=0)


def sum_kernel(in_ref, coadd_ref, mid_ref, chip_ref, next_ref, stack_ref):
    peers = in_ref.shape[0]
    depth = peers * NOTE_LANES
    notes = []
    per_row = LANES // NOTE_LANES
    lane = iota((UNIT, LANES), 1)
    for q in range(peers // per_row):
        total = jnp.zeros((UNIT, LANES), F32)
        for j in range(per_row):
            note = in_ref[q * per_row + j, NOTE:NOTE + UNIT, :].astype(F32)
            total = jnp.where(lane // NOTE_LANES == j, roll(note, j * NOTE_LANES), total)
        notes.append(total)
    notes = jnp.concatenate(notes, axis=1)
    weight, block, peer_weight = notes[0:1], notes[1:2], notes[2:3]
    same = iota((UNIT, depth), 0) == iota((UNIT, depth), 1) % UNIT
    spread = jnp.concatenate(
        [jnp.where(same, jnp.where(block == b, weight, 0.0), 0.0) for b in range(SPT)], axis=0
    ).astype(BF)
    parts = []
    for g in range(R // UNIT):
        pieces = [
            in_ref[v, slot * R + g * UNIT:slot * R + (g + 1) * UNIT, :]
            for v in range(peers) for slot in range(SLOTS)
        ]
        parts.append(jnp.concatenate(pieces, axis=0))
    parts.append(jnp.ones((depth, LANES), BF))
    total = dot(spread, jnp.concatenate(parts, axis=1))
    scale = 1.0 / (total[:, R // UNIT * LANES:] + 1.0)
    for b in range(SPT):
        for g in range(R // UNIT):
            rows = slice(b * UNIT, (b + 1) * UNIT)
            value = total[rows, g * LANES:(g + 1) * LANES] * scale[rows]
            coadd_ref[g * UNIT:(g + 1) * UNIT, b * LANES:(b + 1) * LANES] = value
            stack_ref[(b + 1) * R + g * UNIT:(b + 1) * R + (g + 1) * UNIT, :] = value
    same = iota((NOTE_LANES, depth), 0) == iota((NOTE_LANES, depth), 1) % NOTE_LANES
    edges = jnp.concatenate([in_ref[v, NOTE:MSG, :] for v in range(peers)], axis=0)
    edges = dot(jnp.where(same, peer_weight, 0.0).astype(BF), edges)
    for t in range(2):
        part = edges[t * UNIT:(t + 1) * UNIT]
        counts = edges[UNIT:2 * UNIT]
        left = part * (1.0 / (counts[:, 0:1] + 1.0))
        right = part * (1.0 / (counts[:, 1:2] + 1.0))
        for f in range(2):
            at = (2 * t + f) * UNIT
            stack_ref[at:at + UNIT, :] = roll(left, LANES - HALO - LEFT_AT[f])
            at += (SPT + 1) * R
            stack_ref[at:at + UNIT, :] = roll(right, -RIGHT_AT[f])
    band = taper_bands(3 * LANES, LANES, LANES - HALO)
    high, low = split(stack_ref[...])
    window = jnp.concatenate(
        [
            jnp.concatenate([part[j * R:(j + SPT) * R] for j in range(3)], axis=1)
            for part in (high, low)
        ],
        axis=0,
    )
    mid = dot(window, band, NT)
    mid = (mid[0:SPT * R] + mid[SPT * R:])
    mid = mid[:, 0:LANES] + mid[:, LANES:]
    for s in range(SPT):
        mid_ref[:, s * LANES:(s + 1) * LANES] = mid[s * R:(s + 1) * R]
    even = lax.axis_index("sky") % 2 == 0
    first, last = mid_ref[0:EDGE, :], mid_ref[R - EDGE:R, :]
    chip_ref[...] = jnp.where(even, last, first)
    next_ref[...] = jnp.where(even, first, last)


def down_kernel(mid_ref, chip_ref, next_ref, out_ref):
    norm = sum((1.0 - (a / 21.0) ** 2) ** 2 for a in range(-HALO, HALO + 1))
    even = lax.axis_index("sky") % 2 == 0
    chip, following = chip_ref[...], next_ref[...]
    above, below = jnp.where(even, following, chip), jnp.where(even, chip, following)
    rows = jnp.concatenate([above, mid_ref[...], below], axis=0)
    band = taper_bands(LANES, R, EDGE - HALO)[:, 0:R + 2 * EDGE]
    high, low = split(rows)
    total = dot(jnp.concatenate([band, band], axis=1), jnp.concatenate([high, low], axis=0))
    out_ref[...] = (total[0:R] + total[R:]) * (1.0 / (441.0 * 441.0 * norm))


def vmem(n):
    return [pl.BlockSpec(memory_space=pltpu.VMEM)] * n


GRANT = 56 * 1024 * 1024
PARAMS = pltpu.CompilerParams(vmem_limit_bytes=40 * 1024 * 1024)


def local(
    ccd_tiles, row_taps, col_taps, psf_coeffs, warp_start_x, warp_frac_x, warp_start_y, warp_frac_y,
    tile_weight, strip_owner, strip_block,
):
    peers = lax.axis_size("visit")
    operands = (
        psf_coeffs.transpose(2, 0, 1), tile_weight.reshape(1, 1), strip_owner.reshape(1, SPT), strip_block,
        ccd_tiles, row_taps, col_taps, warp_start_x, warp_frac_x, warp_start_y, warp_frac_y,
    )
    spaces = [pltpu.SMEM, pltpu.VMEM, pltpu.SMEM, pltpu.SMEM] + [pltpu.VMEM] * 7
    messages = pl.pallas_call(
        tile_kernel,
        out_shape=jax.ShapeDtypeStruct((peers, MSG, LANES), BF),
        in_specs=[pl.BlockSpec(memory_space=pltpu.HBM)] * len(operands),
        out_specs=pl.BlockSpec(memory_space=pltpu.VMEM),
        scratch_shapes=[space(x.shape, x.dtype) for space, x in zip(spaces, operands)] + [
            pltpu.SemaphoreType.DMA((len(operands),)),
            pltpu.VMEM((16, 3 * LANES), F32),
            pltpu.VMEM(((SPT + 2) * R, LANES), BF),
            pltpu.VMEM((R, W), F32),
            pltpu.VMEM((6 * R, W), BF),
            pltpu.VMEM((R, W), BF),
            pltpu.SMEM((peers,), jnp.int32),
        ],
        compiler_params=pltpu.CompilerParams(vmem_limit_bytes=GRANT),
    )(*operands)
    received = lax.all_to_all(messages, "visit", 0, 0, tiled=True)
    image = jax.ShapeDtypeStruct((R, W), F32)
    rows = jax.ShapeDtypeStruct((EDGE, W), F32)
    coadd, mid, to_chip, to_next = pl.pallas_call(
        sum_kernel,
        out_shape=(image, image, rows, rows),
        in_specs=vmem(1),
        out_specs=tuple(vmem(4)),
        scratch_shapes=[pltpu.VMEM(((SPT + 2) * R, LANES), F32)],
        compiler_params=PARAMS,
    )(received)
    size = lax.axis_size("sky")
    swap = lambda first: [p for i in range(first, size - 1, 2) for p in ((i, i + 1), (i + 1, i))]
    from_chip = lax.ppermute(to_chip, "sky", swap(0))
    from_next = lax.ppermute(to_next, "sky", swap(1))
    detection = pl.pallas_call(
        down_kernel,
        out_shape=image,
        in_specs=vmem(3),
        out_specs=pl.BlockSpec(memory_space=pltpu.VMEM),
        compiler_params=PARAMS,
    )(mid, from_chip, from_next)
    return coadd, detection


def solution(mesh):
    tiles = ("visit", "sky")
    in_specs = (
        P(tiles, None, None),
        P(),
        P(),
        P(tiles, None, None),
        P(tiles, None),
        P(tiles, None),
        P(tiles, None),
        P(tiles, None),
        P(tiles),
        P(tiles, None, None),
        P(tiles, None),
    )
    out_specs = (P("sky", "visit"), P("sky", "visit"))
    return jax.shard_map(local, mesh=mesh, in_specs=in_specs, out_specs=out_specs, check_vma=False)
```

```python
import jax
import jax.numpy as jnp
from jax import lax
from jax.experimental import pallas as pl
from jax.experimental.pallas import tpu as pltpu
from jax.sharding import PartitionSpec as P

R = 64
W = 2048
NB = 5
KW = 41
HALO = 20
SPT = 16
SLOTS = 2
LANES = 128
UNIT = 16
NOTE = SLOTS * R
AUX = 24
MSG = NOTE + AUX
NOTE_LANES = 2 * UNIT
PLACE = 2 * HALO
NOTE_AT = 2 * PLACE
COUNT_AT = 3 * PLACE
EDGE = 24
NT = (((1,), (1,)), ((), ()))
BF = jnp.bfloat16
F32 = jnp.float32


def dot(left, right, dims=(((1,), (0,)), ((), ()))):
    return lax.dot_general(left, right, dims, preferred_element_type=F32)


def iota(shape, dim):
    return lax.broadcasted_iota(jnp.int32, shape, dim)


def roll(value, shift):
    width = value.shape[1]
    return pltpu.roll(value, shift % width, 1) if shift % width else value


def toeplitz(row, rows, shift=LANES - HALO):
    row = roll(row, shift % 8)
    return pltpu.roll(jnp.broadcast_to(row, (rows, row.shape[1])), shift // 8 * 8, 1, stride=1, stride_axis=0)


def lanczos(offset):
    return (
        3.0
        * jnp.sin(jnp.pi * offset)
        * jnp.sin(jnp.pi * offset / 3.0)
        / (jnp.pi * jnp.pi * offset * offset)
    )


def lanczos_weights(frac):
    shape = (8, frac.shape[1])
    shift = iota(shape, 0) - 2
    return lanczos(jnp.broadcast_to(frac, shape) - shift.astype(F32)).astype(BF).astype(F32)


def tile_kernel(
    coeff_hbm, weight_hbm, owner_hbm, block_hbm,
    tile_hbm, row_taps_hbm, col_taps_hbm, start_x_hbm, frac_x_hbm, start_y_hbm, frac_y_hbm,
    out_ref,
    coeff_ref, weight_ref, owner_ref, block_ref,
    tile_ref, row_taps_ref, col_taps_ref, start_x_ref, frac_x_ref, start_y_ref, frac_y_ref,
    sems, taps_ref, window_ref, matched_ref, source_ref, col_ref, count_ref,
):
    pairs = [
        (row_taps_hbm, row_taps_ref), (tile_hbm, tile_ref), (col_taps_hbm, col_taps_ref),
        (coeff_hbm, coeff_ref), (frac_x_hbm, frac_x_ref), (start_x_hbm, start_x_ref),
        (start_y_hbm, start_y_ref), (frac_y_hbm, frac_y_ref), (weight_hbm, weight_ref),
        (owner_hbm, owner_ref), (block_hbm, block_ref),
    ]
    copies = [pltpu.make_async_copy(src, dst, sems.at[n]) for n, (src, dst) in enumerate(pairs)]
    for copy in copies:
        copy.start()
    taps_ref[...] = jnp.zeros_like(taps_ref)
    peers = out_ref.shape[0]
    for o in range(peers):
        count_ref[o] = 0
    out_ref[...] = jnp.zeros_like(out_ref)
    for copy in copies:
        copy.wait()
    taps_ref[0:NB, 0:KW] = row_taps_ref[...].astype(F32)
    taps_ref[8:8 + NB, 0:KW] = col_taps_ref[...].astype(F32)
    row_band = jnp.concatenate([toeplitz(taps_ref[k:k + 1, :], LANES, 0) for k in range(NB)], axis=0).astype(BF)
    col_bands = [toeplitz(taps_ref[8 + k:9 + k, 0:LANES], R)[:, 0:R].astype(BF) for k in range(NB)]
    moved = roll(tile_ref[0].astype(F32), HALO)
    before = iota((R, LANES), 1) < HALO
    for s in range(SPT + 1):
        strip = moved[:, s % SPT * LANES:(s % SPT + 1) * LANES]
        if s % SPT == 0:
            strip = jnp.where(before == (s > 0), strip, 0.0)
        strip = strip.astype(BF)
        if s < SPT:
            window_ref[s * R:(s + 1) * R, 0:LANES] = strip
        if s > 0:
            window_ref[(s - 1) * R:s * R, LANES:] = strip
    group = 4
    width = group * LANES
    for g in range(SPT // group):
        rows = group * R
        window = window_ref[g * rows:(g + 1) * rows, :]
        across = dot(window, row_band, NT).astype(BF)
        column = iota((1, width), 1) + g * width
        x_coord = (2 * column - (W - 1)).astype(F32) / (W - 1)
        y_coord = (2 * iota((R, 1), 0) - (R - 1)).astype(F32) / (R - 1)
        matched = jnp.zeros((R, width), F32)
        for k in range(NB):
            term = jnp.concatenate(
                [across[j * R:(j + 1) * R, k * LANES:(k + 1) * LANES] for j in range(group)], axis=1
            )
            basis_term = dot(col_bands[k], term)
            coeff_map = coeff_ref[0, 0, k] + coeff_ref[1, 0, k] * x_coord + coeff_ref[2, 0, k] * y_coord
            matched = matched + coeff_map * basis_term
        matched_ref[:, g * width:(g + 1) * width] = matched.astype(BF).astype(F32)
    moved = roll(matched_ref[...], 2)
    for s in range(SPT):
        strip = moved[:, s * LANES:(s + 1) * LANES].astype(BF)
        source_ref[s * R:(s + 1) * R, 0:LANES] = strip
        before = (s - 1) % SPT
        source_ref[before * R:(before + 1) * R, LANES:] = strip
    weights_x = lanczos_weights(frac_x_ref[...])
    chunk = 256
    deep = LANES + 8
    for c in range(W // chunk):
        cols = slice(c * chunk, (c + 1) * chunk)
        start = start_x_ref[:, cols]
        tap = iota((deep, chunk), 0) - start % LANES
        taps = jnp.zeros((deep, chunk), F32)
        for s in range(6):
            taps = jnp.where(tap == s, weights_x[s:s + 1, cols], taps)
        taps = jnp.concatenate([taps, jnp.zeros((2 * LANES - deep, chunk), F32)], axis=0).astype(BF)
        found = dot(source_ref[...], taps)
        total = found[0:R]
        for s in range(1, SPT):
            total = jnp.where(start // LANES == s, found[s * R:(s + 1) * R], total)
        col_ref[:, cols] = total.astype(BF)
    weights_y = lanczos_weights(frac_y_ref[...])
    step = iota((R, R), 0) - start_y_ref[...]
    warp_y = jnp.zeros((R, R), F32)
    for s in range(6):
        warp_y = jnp.where(step == s - 2, weights_y[s:s + 1, :], warp_y)
    warped = dot(warp_y.T.astype(BF), col_ref[...]).astype(BF)
    weight = weight_ref[...].astype(F32)
    row = iota((AUX, LANES), 0)
    lane = iota((AUX, LANES), 1)
    place = lane - NOTE_AT
    last = row - (AUX - 8)
    noted = (last >= 0) & (place >= 0) & (place < NOTE_LANES)
    base = jnp.where(noted & (last == 2), weight, 0.0).astype(BF)
    for o in range(peers):
        out_ref[o, NOTE:MSG, :] = base

    def add(owner, piece):
        out_ref[owner, NOTE:MSG, :] = (out_ref[owner, NOTE:MSG, :].astype(F32) + piece).astype(BF)

    def add_edges(owner, strip, lanes, side):
        strip = strip.astype(F32)
        units = []
        for t in range(AUX // 8):
            at = lane[0:8] - side * HALO
            unit = jnp.where(lane[0:8] == COUNT_AT + side, 1.0, 0.0)
            for f in range(3):
                n = 3 * t + f
                if n < R // 8:
                    part = roll(strip[n * 8:(n + 1) * 8], f * PLACE + side * HALO - lanes)
                    unit = jnp.where((at >= f * PLACE) & (at < f * PLACE + HALO), part, unit)
            units.append(unit)
        add(owner, jnp.concatenate(units, axis=0))

    for s in range(SPT):
        owner, block = owner_ref[0, s], block_ref[0, s]
        slot = count_ref[owner]
        count_ref[owner] = slot + 1
        strip = warped[:, s * LANES:(s + 1) * LANES]
        out_ref[owner, pl.ds(pl.multiple_of(slot * R, R), R), :] = strip
        note = jnp.where(last == 0, weight, jnp.where(last == 1, block.astype(F32), 0.0))
        add(owner, jnp.where(noted & (place // UNIT == slot), note, 0.0))
        pl.when((block == SPT - 1) & (owner < peers - 1))(
            lambda: add_edges(owner + 1, strip, LANES - HALO, 0)
        )
        pl.when((block == 0) & (owner > 0))(lambda: add_edges(owner - 1, strip, 0, 1))


def split(value):
    high = value.astype(BF)
    return high, (value - high.astype(F32)).astype(BF)


def taper_bands(width, rows, shift):
    lane = iota((1, width), 1)
    at = lane - HALO
    taps = jnp.where(lane < KW, 441 - at * at, 0).astype(F32)
    high, low = split(toeplitz(taps, rows, shift))
    return jnp.concatenate([high, low], axis=0)


def sum_kernel(in_ref, coadd_ref, mid_ref, chip_ref, next_ref, stack_ref):
    peers = in_ref.shape[0]
    depth = peers * NOTE_LANES
    aux = [in_ref[v, NOTE:MSG, :].astype(F32) for v in range(peers)]
    notes = []
    per_row = LANES // NOTE_LANES
    lane = iota((8, LANES), 1)
    for q in range(peers // per_row):
        total = jnp.zeros((8, LANES), F32)
        for j in range(per_row):
            note = roll(aux[q * per_row + j][AUX - 8:], j * NOTE_LANES - NOTE_AT)
            total = jnp.where(lane // NOTE_LANES == j, note, total)
        notes.append(total)
    notes = jnp.concatenate(notes, axis=1)
    weight, block, peer_weight = notes[0:1], notes[1:2], notes[2:3]
    same = iota((UNIT, depth), 0) == iota((UNIT, depth), 1) % UNIT
    spread = jnp.concatenate(
        [jnp.where(same, jnp.where(block == b, weight, 0.0), 0.0) for b in range(SPT)], axis=0
    ).astype(BF)
    parts = []
    for g in range(R // UNIT):
        pieces = [
            in_ref[v, slot * R + g * UNIT:slot * R + (g + 1) * UNIT, :]
            for v in range(peers) for slot in range(SLOTS)
        ]
        parts.append(jnp.concatenate(pieces, axis=0))
    parts.append(jnp.ones((depth, LANES), BF))
    total = dot(spread, jnp.concatenate(parts, axis=1))
    scale = 1.0 / (total[:, R // UNIT * LANES:] + 1.0)
    for b in range(SPT):
        for g in range(R // UNIT):
            rows = slice(b * UNIT, (b + 1) * UNIT)
            value = total[rows, g * LANES:(g + 1) * LANES] * scale[rows]
            coadd_ref[g * UNIT:(g + 1) * UNIT, b * LANES:(b + 1) * LANES] = value
            stack_ref[(b + 1) * R + g * UNIT:(b + 1) * R + (g + 1) * UNIT, :] = value
    same = iota((AUX, depth), 0) == iota((AUX, depth), 1) % NOTE_LANES
    gap = jnp.zeros((NOTE_LANES - AUX, LANES), F32)
    edges = jnp.concatenate([x for v in range(peers) for x in (aux[v], gap)], axis=0).astype(BF)
    edges = dot(jnp.where(same, peer_weight, 0.0).astype(BF), edges)
    for side, block in enumerate((0, SPT + 1)):
        sum_weight = edges[AUX - 8:AUX - 7, COUNT_AT + side:COUNT_AT + side + 1]
        value = edges * (1.0 / (sum_weight + 1.0))
        for n in range(R // 8):
            t, f = n // 3, n % 3
            to = (LANES - HALO, 0)[side] - f * PLACE - side * HALO
            stack_ref[block * R + n * 8:block * R + n * 8 + 8, :] = roll(value[t * 8:t * 8 + 8], to)
    band = taper_bands(3 * LANES, LANES, LANES - HALO)
    high, low = split(stack_ref[...])
    window = jnp.concatenate(
        [
            jnp.concatenate([part[j * R:(j + SPT) * R] for j in range(3)], axis=1)
            for part in (high, low)
        ],
        axis=0,
    )
    mid = dot(window, band, NT)
    mid = (mid[0:SPT * R] + mid[SPT * R:])
    mid = mid[:, 0:LANES] + mid[:, LANES:]
    for s in range(SPT):
        mid_ref[:, s * LANES:(s + 1) * LANES] = mid[s * R:(s + 1) * R]
    even = lax.axis_index("sky") % 2 == 0
    first, last = mid_ref[0:EDGE, :], mid_ref[R - EDGE:R, :]
    chip_ref[...] = jnp.where(even, last, first)
    next_ref[...] = jnp.where(even, first, last)


def down_kernel(mid_ref, chip_ref, next_ref, out_ref):
    norm = sum((1.0 - (a / 21.0) ** 2) ** 2 for a in range(-HALO, HALO + 1))
    even = lax.axis_index("sky") % 2 == 0
    chip, following = chip_ref[...], next_ref[...]
    above, below = jnp.where(even, following, chip), jnp.where(even, chip, following)
    rows = jnp.concatenate([above, mid_ref[...], below], axis=0)
    band = taper_bands(LANES, R, EDGE - HALO)[:, 0:R + 2 * EDGE]
    high, low = split(rows)
    total = dot(jnp.concatenate([band, band], axis=1), jnp.concatenate([high, low], axis=0))
    out_ref[...] = (total[0:R] + total[R:]) * (1.0 / (441.0 * 441.0 * norm))


def vmem(n):
    return [pl.BlockSpec(memory_space=pltpu.VMEM)] * n


GRANT = 56 * 1024 * 1024
PARAMS = pltpu.CompilerParams(vmem_limit_bytes=40 * 1024 * 1024)


def tile_call(peers, *operands):
    spaces = [pltpu.SMEM, pltpu.VMEM, pltpu.SMEM, pltpu.SMEM] + [pltpu.VMEM] * 7
    return pl.pallas_call(
        tile_kernel,
        out_shape=jax.ShapeDtypeStruct((peers, MSG, LANES), BF),
        in_specs=[pl.BlockSpec(memory_space=pltpu.HBM)] * len(operands),
        out_specs=pl.BlockSpec(memory_space=pltpu.VMEM),
        scratch_shapes=[space(x.shape, x.dtype) for space, x in zip(spaces, operands)] + [
            pltpu.SemaphoreType.DMA((len(operands),)),
            pltpu.VMEM((16, 2 * LANES), F32),
            pltpu.VMEM((SPT * R, 2 * LANES), BF),
            pltpu.VMEM((R, W), F32),
            pltpu.VMEM((SPT * R, 2 * LANES), BF),
            pltpu.VMEM((R, W), BF),
            pltpu.SMEM((peers,), jnp.int32),
        ],
        compiler_params=pltpu.CompilerParams(vmem_limit_bytes=GRANT),
    )(*operands)


def local(
    ccd_tiles, row_taps, col_taps, psf_coeffs, warp_start_x, warp_frac_x, warp_start_y, warp_frac_y,
    tile_weight, strip_owner, strip_block,
):
    peers = lax.axis_size("visit")
    operands = (
        psf_coeffs.transpose(2, 0, 1), tile_weight.reshape(1, 1), strip_owner.reshape(1, SPT), strip_block,
        ccd_tiles, row_taps, col_taps, warp_start_x, warp_frac_x, warp_start_y, warp_frac_y,
    )
    messages = tile_call(peers, *operands)
    received = lax.all_to_all(messages, "visit", 0, 0, tiled=True)
    image = jax.ShapeDtypeStruct((R, W), F32)
    rows = jax.ShapeDtypeStruct((EDGE, W), F32)
    coadd, mid, to_chip, to_next = pl.pallas_call(
        sum_kernel,
        out_shape=(image, image, rows, rows),
        in_specs=vmem(1),
        out_specs=tuple(vmem(4)),
        scratch_shapes=[pltpu.VMEM(((SPT + 2) * R, LANES), F32)],
        compiler_params=PARAMS,
    )(received)
    size = lax.axis_size("sky")
    swap = lambda first: [p for i in range(first, size - 1, 2) for p in ((i, i + 1), (i + 1, i))]
    from_next = lax.ppermute(to_next, "sky", swap(1))
    from_chip = lax.ppermute(to_chip, "sky", swap(0))
    detection = pl.pallas_call(
        down_kernel,
        out_shape=image,
        in_specs=vmem(3),
        out_specs=pl.BlockSpec(memory_space=pltpu.VMEM),
        compiler_params=PARAMS,
    )(mid, from_chip, from_next)
    return coadd, detection


def solution(mesh):
    tiles = ("visit", "sky")
    in_specs = (
        P(tiles, None, None),
        P(),
        P(),
        P(tiles, None, None),
        P(tiles, None),
        P(tiles, None),
        P(tiles, None),
        P(tiles, None),
        P(tiles),
        P(tiles, None, None),
        P(tiles, None),
    )
    out_specs = (P("sky", "visit"), P("sky", "visit"))
    return jax.shard_map(local, mesh=mesh, in_specs=in_specs, out_specs=out_specs, check_vma=False)
```

```python
import jax
import jax.numpy as jnp
from jax import lax
from jax.experimental import pallas as pl
from jax.experimental.pallas import tpu as pltpu
from jax.sharding import PartitionSpec as P

R = 64
W = 2048
NB = 5
KW = 41
HALO = 20
SPT = 16
SLOTS = 2
LANES = 128
UNIT = 16
NOTE = SLOTS * R
AUX = 24
MSG = NOTE + AUX
NOTE_LANES = 2 * UNIT
PLACE = 2 * HALO
NOTE_AT = 2 * PLACE
COUNT_AT = 3 * PLACE
EDGE = 24
NT = (((1,), (1,)), ((), ()))
BF = jnp.bfloat16
F32 = jnp.float32


def dot(left, right, dims=(((1,), (0,)), ((), ()))):
    return lax.dot_general(left, right, dims, preferred_element_type=F32)


def iota(shape, dim):
    return lax.broadcasted_iota(jnp.int32, shape, dim)


def roll(value, shift):
    width = value.shape[1]
    return pltpu.roll(value, shift % width, 1) if shift % width else value


def toeplitz(row, rows, shift=LANES - HALO):
    row = roll(row, shift % 8)
    return pltpu.roll(jnp.broadcast_to(row, (rows, row.shape[1])), shift // 8 * 8, 1, stride=1, stride_axis=0)


def sin_pi(value):
    folded = jnp.where(value > 0.5, 1.0 - value, jnp.where(value < -0.5, -1.0 - value, value))
    angle = jnp.pi * folded
    square = angle * angle
    total = jnp.full_like(angle, -1.0 / 39916800.0)
    for term in (1.0 / 362880.0, -1.0 / 5040.0, 1.0 / 120.0, -1.0 / 6.0, 1.0):
        total = total * square + term
    return total * angle


def lanczos_weights(frac):
    shape = (8, frac.shape[1])
    shift = iota(shape, 0)
    offset = jnp.broadcast_to(frac, shape) - (shift - 2).astype(F32)
    sine = sin_pi(jnp.broadcast_to(frac, shape))
    sine = jnp.where(shift % 2 == 0, sine, -sine)
    weights = 3.0 * sine * sin_pi(offset * (1.0 / 3.0)) / (jnp.pi * jnp.pi * offset * offset)
    return weights.astype(BF).astype(F32)


def tile_kernel(
    coeff_hbm, weight_hbm, owner_hbm, block_hbm,
    tile_hbm, row_taps_hbm, col_taps_hbm, start_x_hbm, frac_x_hbm, start_y_hbm, frac_y_hbm,
    out_ref,
    coeff_ref, weight_ref, owner_ref, block_ref,
    tile_ref, row_taps_ref, col_taps_ref, start_x_ref, frac_x_ref, start_y_ref, frac_y_ref,
    sems, taps_ref, window_ref, matched_ref, source_ref, col_ref, count_ref,
):
    pairs = [
        (row_taps_hbm, row_taps_ref), (tile_hbm, tile_ref), (col_taps_hbm, col_taps_ref),
        (coeff_hbm, coeff_ref), (frac_x_hbm, frac_x_ref), (start_x_hbm, start_x_ref),
        (start_y_hbm, start_y_ref), (frac_y_hbm, frac_y_ref), (weight_hbm, weight_ref),
        (owner_hbm, owner_ref), (block_hbm, block_ref),
    ]
    copies = [pltpu.make_async_copy(src, dst, sems.at[n]) for n, (src, dst) in enumerate(pairs)]
    for copy in copies:
        copy.start()
    taps_ref[...] = jnp.zeros_like(taps_ref)
    peers = out_ref.shape[0]
    for o in range(peers):
        count_ref[o] = 0
    out_ref[...] = jnp.zeros_like(out_ref)
    for copy in copies:
        copy.wait()
    taps_ref[0:NB, 0:KW] = row_taps_ref[...].astype(F32)
    taps_ref[8:8 + NB, 0:KW] = col_taps_ref[...].astype(F32)
    row_band = jnp.concatenate([toeplitz(taps_ref[k:k + 1, :], LANES, 0) for k in range(NB)], axis=0).astype(BF)
    col_bands = [toeplitz(taps_ref[8 + k:9 + k, 0:LANES], R)[:, 0:R].astype(BF) for k in range(NB)]
    moved = roll(tile_ref[0].astype(F32), HALO)
    before = iota((R, LANES), 1) < HALO
    for s in range(SPT + 1):
        strip = moved[:, s % SPT * LANES:(s % SPT + 1) * LANES]
        if s % SPT == 0:
            strip = jnp.where(before == (s > 0), strip, 0.0)
        strip = strip.astype(BF)
        if s < SPT:
            window_ref[s * R:(s + 1) * R, 0:LANES] = strip
        if s > 0:
            window_ref[(s - 1) * R:s * R, LANES:] = strip
    group = 16
    width = group * LANES
    for g in range(SPT // group):
        rows = group * R
        window = window_ref[g * rows:(g + 1) * rows, :]
        across = dot(window, row_band, NT).astype(BF)
        column = iota((1, width), 1) + g * width
        x_coord = (2 * column - (W - 1)).astype(F32) / (W - 1)
        y_coord = (2 * iota((R, 1), 0) - (R - 1)).astype(F32) / (R - 1)
        matched = jnp.zeros((R, width), F32)
        for k in range(NB):
            term = jnp.concatenate(
                [across[j * R:(j + 1) * R, k * LANES:(k + 1) * LANES] for j in range(group)], axis=1
            )
            basis_term = dot(col_bands[k], term)
            coeff_map = coeff_ref[0, 0, k] + coeff_ref[1, 0, k] * x_coord + coeff_ref[2, 0, k] * y_coord
            matched = matched + coeff_map * basis_term
        matched_ref[:, g * width:(g + 1) * width] = matched.astype(BF).astype(F32)
    moved = roll(matched_ref[...], 2)
    for s in range(SPT):
        strip = moved[:, s * LANES:(s + 1) * LANES].astype(BF)
        source_ref[s * R:(s + 1) * R, 0:LANES] = strip
        before = (s - 1) % SPT
        source_ref[before * R:(before + 1) * R, LANES:] = strip
    weights_x = lanczos_weights(frac_x_ref[...])
    chunk = 512
    deep = LANES + 16
    order = iota((deep, chunk), 0).astype(F32).astype(BF)
    for c in range(W // chunk):
        cols = slice(c * chunk, (c + 1) * chunk)
        start = start_x_ref[:, cols]
        tap = order - (start % LANES).astype(F32).astype(BF)
        taps = jnp.zeros((deep, chunk), BF)
        for s in range(6):
            taps = jnp.where(tap == s, weights_x[s:s + 1, cols].astype(BF), taps)
        taps = jnp.concatenate([taps, jnp.zeros((2 * LANES - deep, chunk), BF)], axis=0)
        found = dot(source_ref[...], taps)
        place = jnp.broadcast_to(start // LANES, (8, chunk))
        total = found[0:R].reshape(R // 8, 8, chunk)
        for s in range(1, SPT):
            part = found[s * R:(s + 1) * R].reshape(R // 8, 8, chunk)
            total = jnp.where((place == s)[None], part, total)
        col_ref[:, cols] = total.reshape(R, chunk).astype(BF)
    weights_y = lanczos_weights(frac_y_ref[...])
    step = iota((R, R), 0) - start_y_ref[...]
    warp_y = jnp.zeros((R, R), F32)
    for s in range(6):
        warp_y = jnp.where(step == s - 2, weights_y[s:s + 1, :], warp_y)
    warped = dot(warp_y.T.astype(BF), col_ref[...]).astype(BF)
    weight = weight_ref[...].astype(F32)
    row = iota((AUX, LANES), 0)
    lane = iota((AUX, LANES), 1)
    place = lane - NOTE_AT
    last = row - (AUX - 8)
    noted = (last >= 0) & (place >= 0) & (place < NOTE_LANES)
    base = jnp.where(noted & (last == 2), weight, 0.0).astype(BF)
    for o in range(peers):
        out_ref[o, NOTE:MSG, :] = base

    def add(owner, piece):
        out_ref[owner, NOTE:MSG, :] = (out_ref[owner, NOTE:MSG, :].astype(F32) + piece).astype(BF)

    def add_edges(owner, strip, lanes, side):
        strip = strip.astype(F32)
        units = []
        for t in range(AUX // 8):
            at = lane[0:8] - side * HALO
            unit = jnp.where(lane[0:8] == COUNT_AT + side, 1.0, 0.0)
            for f in range(3):
                n = 3 * t + f
                if n < R // 8:
                    part = roll(strip[n * 8:(n + 1) * 8], f * PLACE + side * HALO - lanes)
                    unit = jnp.where((at >= f * PLACE) & (at < f * PLACE + HALO), part, unit)
            units.append(unit)
        add(owner, jnp.concatenate(units, axis=0))

    for s in range(SPT):
        owner, block = owner_ref[0, s], block_ref[0, s]
        slot = count_ref[owner]
        count_ref[owner] = slot + 1
        strip = warped[:, s * LANES:(s + 1) * LANES]
        out_ref[owner, pl.ds(pl.multiple_of(slot * R, R), R), :] = strip
        note = jnp.where(last == 0, weight, jnp.where(last == 1, block.astype(F32), 0.0))
        add(owner, jnp.where(noted & (place // UNIT == slot), note, 0.0))

        @pl.when((block == SPT - 1) | (block == 0))
        def _():
            pl.when((block > 0) & (owner < peers - 1))(
                lambda: add_edges(owner + 1, strip, LANES - HALO, 0)
            )
            pl.when((block == 0) & (owner > 0))(lambda: add_edges(owner - 1, strip, 0, 1))


def split(value):
    high = value.astype(BF)
    return high, (value - high.astype(F32)).astype(BF)


def taper_bands(width, rows, shift):
    lane = iota((1, width), 1)
    at = lane - HALO
    taps = jnp.where(lane < KW, 441 - at * at, 0).astype(F32)
    high, low = split(toeplitz(taps, rows, shift))
    return jnp.concatenate([high, low], axis=0)


def sum_kernel(in_ref, coadd_ref, mid_ref, chip_ref, next_ref, stack_ref):
    peers = in_ref.shape[0]
    depth = peers * NOTE_LANES
    aux = [in_ref[v, NOTE:MSG, :].astype(F32) for v in range(peers)]
    notes = []
    per_row = LANES // NOTE_LANES
    lane = iota((8, LANES), 1)
    for q in range(peers // per_row):
        total = jnp.zeros((8, LANES), F32)
        for j in range(per_row):
            note = roll(aux[q * per_row + j][AUX - 8:], j * NOTE_LANES - NOTE_AT)
            total = jnp.where(lane // NOTE_LANES == j, note, total)
        notes.append(total)
    notes = jnp.concatenate(notes, axis=1)
    weight, block, peer_weight = notes[0:1], notes[1:2], notes[2:3]
    same = iota((UNIT, depth), 0) == iota((UNIT, depth), 1) % UNIT
    spread = jnp.concatenate(
        [jnp.where(same, jnp.where(block == b, weight, 0.0), 0.0) for b in range(SPT)], axis=0
    ).astype(BF)
    parts = []
    for g in range(R // UNIT):
        pieces = [
            in_ref[v, slot * R + g * UNIT:slot * R + (g + 1) * UNIT, :]
            for v in range(peers) for slot in range(SLOTS)
        ]
        parts.append(jnp.concatenate(pieces, axis=0))
    parts.append(jnp.ones((depth, LANES), BF))
    total = dot(spread, jnp.concatenate(parts, axis=1))
    scale = 1.0 / (total[:, R // UNIT * LANES:] + 1.0)
    for b in range(SPT):
        for g in range(R // UNIT):
            rows = slice(b * UNIT, (b + 1) * UNIT)
            value = total[rows, g * LANES:(g + 1) * LANES] * scale[rows]
            coadd_ref[g * UNIT:(g + 1) * UNIT, b * LANES:(b + 1) * LANES] = value
            stack_ref[(b + 1) * R + g * UNIT:(b + 1) * R + (g + 1) * UNIT, :] = value
    same = iota((AUX, depth), 0) == iota((AUX, depth), 1) % NOTE_LANES
    gap = jnp.zeros((NOTE_LANES - AUX, LANES), F32)
    edges = jnp.concatenate([x for v in range(peers) for x in (aux[v], gap)], axis=0).astype(BF)
    edges = dot(jnp.where(same, peer_weight, 0.0).astype(BF), edges)
    for side, block in enumerate((0, SPT + 1)):
        sum_weight = edges[AUX - 8:AUX - 7, COUNT_AT + side:COUNT_AT + side + 1]
        value = edges * (1.0 / (sum_weight + 1.0))
        for n in range(R // 8):
            t, f = n // 3, n % 3
            to = (LANES - HALO, 0)[side] - f * PLACE - side * HALO
            stack_ref[block * R + n * 8:block * R + n * 8 + 8, :] = roll(value[t * 8:t * 8 + 8], to)
    band = taper_bands(3 * LANES, LANES, LANES - HALO)
    high, low = split(stack_ref[...])
    window = jnp.concatenate(
        [
            jnp.concatenate([part[j * R:(j + SPT) * R] for j in range(3)], axis=1)
            for part in (high, low)
        ],
        axis=0,
    )
    mid = dot(window, band, NT)
    mid = (mid[0:SPT * R] + mid[SPT * R:])
    mid = mid[:, 0:LANES] + mid[:, LANES:]
    for s in range(SPT):
        mid_ref[:, s * LANES:(s + 1) * LANES] = mid[s * R:(s + 1) * R]
    even = lax.axis_index("sky") % 2 == 0
    first, last = mid_ref[0:EDGE, :], mid_ref[R - EDGE:R, :]
    chip_ref[...] = jnp.where(even, last, first).astype(BF)
    next_ref[...] = jnp.where(even, first, last).astype(BF)


def down_kernel(mid_ref, chip_ref, next_ref, out_ref):
    norm = sum((1.0 - (a / 21.0) ** 2) ** 2 for a in range(-HALO, HALO + 1))
    even = lax.axis_index("sky") % 2 == 0
    chip, following = chip_ref[...].astype(F32), next_ref[...].astype(F32)
    above, below = jnp.where(even, following, chip), jnp.where(even, chip, following)
    rows = jnp.concatenate([above, mid_ref[...], below], axis=0)
    band = taper_bands(LANES, R, EDGE - HALO)[:, 0:R + 2 * EDGE]
    high, low = split(rows)
    total = dot(jnp.concatenate([band, band], axis=1), jnp.concatenate([high, low], axis=0))
    out_ref[...] = (total[0:R] + total[R:]) * (1.0 / (441.0 * 441.0 * norm))


def vmem(n):
    return [pl.BlockSpec(memory_space=pltpu.VMEM)] * n


GRANT = 56 * 1024 * 1024
PARAMS = pltpu.CompilerParams(vmem_limit_bytes=40 * 1024 * 1024)


def tile_call(peers, *operands):
    spaces = [pltpu.SMEM, pltpu.VMEM, pltpu.SMEM, pltpu.SMEM] + [pltpu.VMEM] * 7
    return pl.pallas_call(
        tile_kernel,
        out_shape=jax.ShapeDtypeStruct((peers, MSG, LANES), BF),
        in_specs=[pl.BlockSpec(memory_space=pltpu.HBM)] * len(operands),
        out_specs=pl.BlockSpec(memory_space=pltpu.VMEM),
        scratch_shapes=[space(x.shape, x.dtype) for space, x in zip(spaces, operands)] + [
            pltpu.SemaphoreType.DMA((len(operands),)),
            pltpu.VMEM((16, 2 * LANES), F32),
            pltpu.VMEM((SPT * R, 2 * LANES), BF),
            pltpu.VMEM((R, W), F32),
            pltpu.VMEM((SPT * R, 2 * LANES), BF),
            pltpu.VMEM((R, W), BF),
            pltpu.SMEM((peers,), jnp.int32),
        ],
        compiler_params=pltpu.CompilerParams(vmem_limit_bytes=GRANT),
    )(*operands)


def sum_call(received):
    image = jax.ShapeDtypeStruct((R, W), F32)
    rows = jax.ShapeDtypeStruct((EDGE, W), BF)
    return pl.pallas_call(
        sum_kernel,
        out_shape=(image, image, rows, rows),
        in_specs=vmem(1),
        out_specs=tuple(vmem(4)),
        scratch_shapes=[pltpu.VMEM(((SPT + 2) * R, LANES), F32)],
        compiler_params=PARAMS,
    )(received)


def down_call(mid, from_chip, from_next):
    return pl.pallas_call(
        down_kernel,
        out_shape=jax.ShapeDtypeStruct((R, W), F32),
        in_specs=vmem(3),
        out_specs=pl.BlockSpec(memory_space=pltpu.VMEM),
        compiler_params=PARAMS,
    )(mid, from_chip, from_next)


def local(
    ccd_tiles, row_taps, col_taps, psf_coeffs, warp_start_x, warp_frac_x, warp_start_y, warp_frac_y,
    tile_weight, strip_owner, strip_block,
):
    peers = lax.axis_size("visit")
    operands = (
        psf_coeffs.transpose(2, 0, 1), tile_weight.reshape(1, 1), strip_owner.reshape(1, SPT), strip_block,
        ccd_tiles, row_taps, col_taps, warp_start_x, warp_frac_x, warp_start_y, warp_frac_y,
    )
    messages = tile_call(peers, *operands)
    received = lax.all_to_all(messages, "visit", 0, 0, tiled=True)
    coadd, mid, to_chip, to_next = sum_call(received)
    size = lax.axis_size("sky")
    swap = lambda first: [p for i in range(first, size - 1, 2) for p in ((i, i + 1), (i + 1, i))]
    from_next = lax.ppermute(to_next, "sky", swap(1))
    from_chip = lax.ppermute(to_chip, "sky", swap(0))
    detection = down_call(mid, from_chip, from_next)
    return coadd, detection


def solution(mesh):
    tiles = ("visit", "sky")
    in_specs = (
        P(tiles, None, None),
        P(),
        P(),
        P(tiles, None, None),
        P(tiles, None),
        P(tiles, None),
        P(tiles, None),
        P(tiles, None),
        P(tiles),
        P(tiles, None, None),
        P(tiles, None),
    )
    out_specs = (P("sky", "visit"), P("sky", "visit"))
    return jax.shard_map(local, mesh=mesh, in_specs=in_specs, out_specs=out_specs, check_vma=False)
```

```python
import jax
import jax.numpy as jnp
from jax import lax
from jax.experimental import pallas as pl
from jax.experimental.pallas import tpu as pltpu
from jax.sharding import PartitionSpec as P

R = 64
W = 2048
NB = 5
KW = 41
HALO = 20
SPT = 16
SLOTS = 2
LANES = 128
UNIT = 16
NOTE = SLOTS * R
AUX = 24
MSG = NOTE + AUX
NOTE_LANES = 2 * UNIT
PLACE = 2 * HALO
NOTE_AT = 2 * PLACE
COUNT_AT = 3 * PLACE
EDGE = 24
NT = (((1,), (1,)), ((), ()))
BF = jnp.bfloat16
F32 = jnp.float32


def dot(left, right, dims=(((1,), (0,)), ((), ()))):
    return lax.dot_general(left, right, dims, preferred_element_type=F32)


def iota(shape, dim):
    return lax.broadcasted_iota(jnp.int32, shape, dim)


def roll(value, shift):
    width = value.shape[1]
    return pltpu.roll(value, shift % width, 1) if shift % width else value


def toeplitz(row, rows, shift=LANES - HALO):
    row = roll(row, shift % 8)
    return pltpu.roll(jnp.broadcast_to(row, (rows, row.shape[1])), shift // 8 * 8, 1, stride=1, stride_axis=0)


def sin_pi(value):
    folded = jnp.where(value > 0.5, 1.0 - value, jnp.where(value < -0.5, -1.0 - value, value))
    angle = jnp.pi * folded
    square = angle * angle
    total = jnp.full_like(angle, -1.0 / 39916800.0)
    for term in (1.0 / 362880.0, -1.0 / 5040.0, 1.0 / 120.0, -1.0 / 6.0, 1.0):
        total = total * square + term
    return total * angle


def lanczos_weights(frac):
    shape = (8, frac.shape[1])
    shift = iota(shape, 0)
    offset = jnp.broadcast_to(frac, shape) - (shift - 2).astype(F32)
    sine = sin_pi(jnp.broadcast_to(frac, shape))
    sine = jnp.where(shift % 2 == 0, sine, -sine)
    weights = 3.0 * sine * sin_pi(offset * (1.0 / 3.0)) / (jnp.pi * jnp.pi * offset * offset)
    return weights.astype(BF).astype(F32)


def tile_kernel(
    coeff_hbm, weight_hbm, owner_hbm, block_hbm,
    tile_hbm, row_taps_hbm, col_taps_hbm, start_x_hbm, frac_x_hbm, start_y_hbm, frac_y_hbm,
    out_ref,
    coeff_ref, weight_ref, owner_ref, block_ref,
    tile_ref, row_taps_ref, col_taps_ref, start_x_ref, frac_x_ref, start_y_ref, frac_y_ref,
    sems, taps_ref, window_ref, matched_ref, source_ref, col_ref, count_ref,
):
    pairs = [
        (row_taps_hbm, row_taps_ref), (tile_hbm, tile_ref), (col_taps_hbm, col_taps_ref),
        (coeff_hbm, coeff_ref), (frac_x_hbm, frac_x_ref), (start_x_hbm, start_x_ref),
        (start_y_hbm, start_y_ref), (frac_y_hbm, frac_y_ref), (weight_hbm, weight_ref),
        (owner_hbm, owner_ref), (block_hbm, block_ref),
    ]
    copies = [pltpu.make_async_copy(src, dst, sems.at[n]) for n, (src, dst) in enumerate(pairs)]
    for copy in copies:
        copy.start()
    taps_ref[...] = jnp.zeros_like(taps_ref)
    peers = out_ref.shape[0]
    for o in range(peers):
        count_ref[o] = 0
    out_ref[...] = jnp.zeros_like(out_ref)
    for copy in copies:
        copy.wait()
    taps_ref[0:NB, 0:KW] = row_taps_ref[...].astype(F32)
    taps_ref[8:8 + NB, 0:KW] = col_taps_ref[...].astype(F32)
    row_band = jnp.concatenate([toeplitz(taps_ref[k:k + 1, :], LANES, 0) for k in range(NB)], axis=0).astype(BF)
    col_bands = [toeplitz(taps_ref[8 + k:9 + k, 0:LANES], R)[:, 0:R].astype(BF) for k in range(NB)]
    moved = roll(tile_ref[0].astype(F32), HALO)
    before = iota((R, LANES), 1) < HALO
    for s in range(SPT + 1):
        strip = moved[:, s % SPT * LANES:(s % SPT + 1) * LANES]
        if s % SPT == 0:
            strip = jnp.where(before == (s > 0), strip, 0.0)
        strip = strip.astype(BF)
        if s < SPT:
            window_ref[s * R:(s + 1) * R, 0:LANES] = strip
        if s > 0:
            window_ref[(s - 1) * R:s * R, LANES:] = strip
    group = 16
    width = group * LANES
    for g in range(SPT // group):
        rows = group * R
        window = window_ref[g * rows:(g + 1) * rows, :]
        across = dot(window, row_band, NT).astype(BF)
        column = iota((1, width), 1) + g * width
        x_coord = (2 * column - (W - 1)).astype(F32) / (W - 1)
        y_coord = (2 * iota((R, 1), 0) - (R - 1)).astype(F32) / (R - 1)
        matched = jnp.zeros((R, width), F32)
        for k in range(NB):
            term = jnp.concatenate(
                [across[j * R:(j + 1) * R, k * LANES:(k + 1) * LANES] for j in range(group)], axis=1
            )
            basis_term = dot(col_bands[k], term)
            coeff_map = coeff_ref[0, 0, k] + coeff_ref[1, 0, k] * x_coord + coeff_ref[2, 0, k] * y_coord
            matched = matched + coeff_map * basis_term
        matched_ref[:, g * width:(g + 1) * width] = matched.astype(BF).astype(F32)
    moved = roll(matched_ref[...], 2)
    for s in range(SPT):
        strip = moved[:, s * LANES:(s + 1) * LANES].astype(BF)
        source_ref[s * R:(s + 1) * R, 0:LANES] = strip
        before = (s - 1) % SPT
        source_ref[before * R:(before + 1) * R, LANES:] = strip
    weights_x = lanczos_weights(frac_x_ref[...])
    chunk = 512
    deep = LANES + 16
    order = iota((deep, chunk), 0).astype(F32).astype(BF)
    for c in range(W // chunk):
        cols = slice(c * chunk, (c + 1) * chunk)
        start = start_x_ref[:, cols]
        tap = order - (start % LANES).astype(F32).astype(BF)
        taps = jnp.zeros((deep, chunk), BF)
        for s in range(6):
            taps = jnp.where(tap == s, weights_x[s:s + 1, cols].astype(BF), taps)
        taps = jnp.concatenate([taps, jnp.zeros((2 * LANES - deep, chunk), BF)], axis=0)
        found = dot(source_ref[...], taps)
        place = jnp.broadcast_to(start // LANES, (8, chunk))
        total = found[0:R].reshape(R // 8, 8, chunk)
        for s in range(1, SPT):
            part = found[s * R:(s + 1) * R].reshape(R // 8, 8, chunk)
            total = jnp.where((place == s)[None], part, total)
        col_ref[:, cols] = total.reshape(R, chunk).astype(BF)
    weights_y = lanczos_weights(frac_y_ref[...])
    step = iota((R, R), 0) - start_y_ref[...]
    warp_y = jnp.zeros((R, R), F32)
    for s in range(6):
        warp_y = jnp.where(step == s - 2, weights_y[s:s + 1, :], warp_y)
    warped = dot(warp_y.T.astype(BF), col_ref[...]).astype(BF)
    weight = weight_ref[...].astype(F32)
    row = iota((AUX, LANES), 0)
    lane = iota((AUX, LANES), 1)
    place = lane - NOTE_AT
    last = row - (AUX - 8)
    noted = (last >= 0) & (place >= 0) & (place < NOTE_LANES)
    base = jnp.where(noted & (last == 2), weight, 0.0).astype(BF)
    for o in range(peers):
        out_ref[o, NOTE:MSG, :] = base

    def add(owner, piece):
        out_ref[owner, NOTE:MSG, :] = (out_ref[owner, NOTE:MSG, :].astype(F32) + piece).astype(BF)

    def add_edges(owner, strip, lanes, side):
        strip = strip.astype(F32)
        units = []
        for t in range(AUX // 8):
            at = lane[0:8] - side * HALO
            unit = jnp.where(lane[0:8] == COUNT_AT + side, 1.0, 0.0)
            for f in range(3):
                n = 3 * t + f
                if n < R // 8:
                    part = roll(strip[n * 8:(n + 1) * 8], f * PLACE + side * HALO - lanes)
                    unit = jnp.where((at >= f * PLACE) & (at < f * PLACE + HALO), part, unit)
            units.append(unit)
        add(owner, jnp.concatenate(units, axis=0))

    for s in range(SPT):
        owner, block = owner_ref[0, s], block_ref[0, s]
        slot = count_ref[owner]
        count_ref[owner] = slot + 1
        strip = warped[:, s * LANES:(s + 1) * LANES]
        out_ref[owner, pl.ds(pl.multiple_of(slot * R, R), R), :] = strip
        note = jnp.where(last == 0, weight, jnp.where(last == 1, block.astype(F32), 0.0))
        add(owner, jnp.where(noted & (place // UNIT == slot), note, 0.0))

        @pl.when((block == SPT - 1) | (block == 0))
        def _():
            pl.when((block > 0) & (owner < peers - 1))(
                lambda: add_edges(owner + 1, strip, LANES - HALO, 0)
            )
            pl.when((block == 0) & (owner > 0))(lambda: add_edges(owner - 1, strip, 0, 1))


def split(value):
    high = value.astype(BF)
    return high, (value - high.astype(F32)).astype(BF)


def taper_bands(width, rows, shift):
    lane = iota((1, width), 1)
    at = lane - HALO
    taps = jnp.where(lane < KW, 441 - at * at, 0).astype(F32)
    high, low = split(toeplitz(taps, rows, shift))
    return jnp.concatenate([high, low], axis=0)


def band_kernel(across_ref, down_ref):
    across_ref[...] = taper_bands(3 * LANES, LANES, LANES - HALO)
    down_ref[...] = taper_bands(LANES, R, EDGE - HALO)


def sum_kernel(in_ref, band_ref, coadd_ref, mid_ref, chip_ref, next_ref, stack_ref):
    peers = in_ref.shape[0]
    depth = peers * NOTE_LANES
    aux = [in_ref[v, NOTE:MSG, :].astype(F32) for v in range(peers)]
    notes = []
    per_row = LANES // NOTE_LANES
    lane = iota((8, LANES), 1)
    for q in range(peers // per_row):
        total = jnp.zeros((8, LANES), F32)
        for j in range(per_row):
            note = roll(aux[q * per_row + j][AUX - 8:], j * NOTE_LANES - NOTE_AT)
            total = jnp.where(lane // NOTE_LANES == j, note, total)
        notes.append(total)
    notes = jnp.concatenate(notes, axis=1)
    weight, block, peer_weight = notes[0:1], notes[1:2], notes[2:3]
    same = iota((UNIT, depth), 0) == iota((UNIT, depth), 1) % UNIT
    spread = jnp.concatenate(
        [jnp.where(same, jnp.where(block == b, weight, 0.0), 0.0) for b in range(SPT)], axis=0
    ).astype(BF)
    parts = []
    for g in range(R // UNIT):
        pieces = [
            in_ref[v, slot * R + g * UNIT:slot * R + (g + 1) * UNIT, :]
            for v in range(peers) for slot in range(SLOTS)
        ]
        parts.append(jnp.concatenate(pieces, axis=0))
    parts.append(jnp.ones((depth, LANES), BF))
    total = dot(spread, jnp.concatenate(parts, axis=1))
    scale = 1.0 / (total[:, R // UNIT * LANES:] + 1.0)
    for b in range(SPT):
        for g in range(R // UNIT):
            rows = slice(b * UNIT, (b + 1) * UNIT)
            value = total[rows, g * LANES:(g + 1) * LANES] * scale[rows]
            coadd_ref[g * UNIT:(g + 1) * UNIT, b * LANES:(b + 1) * LANES] = value
            stack_ref[(b + 1) * R + g * UNIT:(b + 1) * R + (g + 1) * UNIT, :] = value
    same = iota((AUX, depth), 0) == iota((AUX, depth), 1) % NOTE_LANES
    gap = jnp.zeros((NOTE_LANES - AUX, LANES), F32)
    edges = jnp.concatenate([x for v in range(peers) for x in (aux[v], gap)], axis=0).astype(BF)
    edges = dot(jnp.where(same, peer_weight, 0.0).astype(BF), edges)
    for side, block in enumerate((0, SPT + 1)):
        sum_weight = edges[AUX - 8:AUX - 7, COUNT_AT + side:COUNT_AT + side + 1]
        value = edges * (1.0 / (sum_weight + 1.0))
        for n in range(R // 8):
            t, f = n // 3, n % 3
            to = (LANES - HALO, 0)[side] - f * PLACE - side * HALO
            stack_ref[block * R + n * 8:block * R + n * 8 + 8, :] = roll(value[t * 8:t * 8 + 8], to)
    band = band_ref[...]
    high, low = split(stack_ref[...])
    window = jnp.concatenate(
        [
            jnp.concatenate([part[j * R:(j + SPT) * R] for j in range(3)], axis=1)
            for part in (high, low)
        ],
        axis=0,
    )
    mid = dot(window, band, NT)
    mid = (mid[0:SPT * R] + mid[SPT * R:])
    mid = mid[:, 0:LANES] + mid[:, LANES:]
    for s in range(SPT):
        mid_ref[:, s * LANES:(s + 1) * LANES] = mid[s * R:(s + 1) * R]
    even = lax.axis_index("sky") % 2 == 0
    first, last = mid_ref[0:EDGE, :], mid_ref[R - EDGE:R, :]
    chip_ref[...] = jnp.where(even, last, first).astype(BF)
    next_ref[...] = jnp.where(even, first, last).astype(BF)


def down_kernel(mid_ref, chip_ref, next_ref, band_ref, out_ref):
    norm = sum((1.0 - (a / 21.0) ** 2) ** 2 for a in range(-HALO, HALO + 1))
    even = lax.axis_index("sky") % 2 == 0
    chip, following = chip_ref[...].astype(F32), next_ref[...].astype(F32)
    above, below = jnp.where(even, following, chip), jnp.where(even, chip, following)
    rows = jnp.concatenate([above, mid_ref[...], below], axis=0)
    band = band_ref[:, 0:R + 2 * EDGE]
    high, low = split(rows)
    total = dot(jnp.concatenate([band, band], axis=1), jnp.concatenate([high, low], axis=0))
    out_ref[...] = (total[0:R] + total[R:]) * (1.0 / (441.0 * 441.0 * norm))


def vmem(n):
    return [pl.BlockSpec(memory_space=pltpu.VMEM)] * n


GRANT = 56 * 1024 * 1024
PARAMS = pltpu.CompilerParams(vmem_limit_bytes=40 * 1024 * 1024)


def tile_call(peers, *operands):
    spaces = [pltpu.SMEM, pltpu.VMEM, pltpu.SMEM, pltpu.SMEM] + [pltpu.VMEM] * 7
    return pl.pallas_call(
        tile_kernel,
        out_shape=jax.ShapeDtypeStruct((peers, MSG, LANES), BF),
        in_specs=[pl.BlockSpec(memory_space=pltpu.HBM)] * len(operands),
        out_specs=pl.BlockSpec(memory_space=pltpu.VMEM),
        scratch_shapes=[space(x.shape, x.dtype) for space, x in zip(spaces, operands)] + [
            pltpu.SemaphoreType.DMA((len(operands),)),
            pltpu.VMEM((16, 2 * LANES), F32),
            pltpu.VMEM((SPT * R, 2 * LANES), BF),
            pltpu.VMEM((R, W), F32),
            pltpu.VMEM((SPT * R, 2 * LANES), BF),
            pltpu.VMEM((R, W), BF),
            pltpu.SMEM((peers,), jnp.int32),
        ],
        compiler_params=pltpu.CompilerParams(vmem_limit_bytes=GRANT),
    )(*operands)


def sum_call(received, band):
    image = jax.ShapeDtypeStruct((R, W), F32)
    rows = jax.ShapeDtypeStruct((EDGE, W), BF)
    return pl.pallas_call(
        sum_kernel,
        out_shape=(image, image, rows, rows),
        in_specs=vmem(2),
        out_specs=tuple(vmem(4)),
        scratch_shapes=[pltpu.VMEM(((SPT + 2) * R, LANES), F32)],
        compiler_params=PARAMS,
    )(received, band)


def down_call(mid, from_chip, from_next, band):
    return pl.pallas_call(
        down_kernel,
        out_shape=jax.ShapeDtypeStruct((R, W), F32),
        in_specs=vmem(4),
        out_specs=pl.BlockSpec(memory_space=pltpu.VMEM),
        compiler_params=PARAMS,
    )(mid, from_chip, from_next, band)


def local(
    ccd_tiles, row_taps, col_taps, psf_coeffs, warp_start_x, warp_frac_x, warp_start_y, warp_frac_y,
    tile_weight, strip_owner, strip_block,
):
    peers = lax.axis_size("visit")
    operands = (
        psf_coeffs.transpose(2, 0, 1), tile_weight.reshape(1, 1), strip_owner.reshape(1, SPT), strip_block,
        ccd_tiles, row_taps, col_taps, warp_start_x, warp_frac_x, warp_start_y, warp_frac_y,
    )
    messages = tile_call(peers, *operands)
    band_across, band_down = pl.pallas_call(
        band_kernel,
        out_shape=(jax.ShapeDtypeStruct((2 * LANES, 3 * LANES), BF), jax.ShapeDtypeStruct((2 * R, LANES), BF)),
        out_specs=tuple(vmem(2)),
        compiler_params=PARAMS,
    )()
    received = lax.all_to_all(messages, "visit", 0, 0, tiled=True)
    coadd, mid, to_chip, to_next = sum_call(received, band_across)
    size = lax.axis_size("sky")
    swap = lambda first: [p for i in range(first, size - 1, 2) for p in ((i, i + 1), (i + 1, i))]
    from_next = lax.ppermute(to_next, "sky", swap(1))
    from_chip = lax.ppermute(to_chip, "sky", swap(0))
    detection = down_call(mid, from_chip, from_next, band_down)
    return coadd, detection


def solution(mesh):
    tiles = ("visit", "sky")
    in_specs = (
        P(tiles, None, None),
        P(),
        P(),
        P(tiles, None, None),
        P(tiles, None),
        P(tiles, None),
        P(tiles, None),
        P(tiles, None),
        P(tiles),
        P(tiles, None, None),
        P(tiles, None),
    )
    out_specs = (P("sky", "visit"), P("sky", "visit"))
    return jax.shard_map(local, mesh=mesh, in_specs=in_specs, out_specs=out_specs, check_vma=False)
```

```python
import jax
import jax.numpy as jnp
from jax import lax
from jax.experimental import pallas as pl
from jax.experimental.pallas import tpu as pltpu
from jax.sharding import PartitionSpec as P

R = 64
W = 2048
NB = 5
KW = 41
HALO = 20
SPT = 16
SLOTS = 2
LANES = 128
UNIT = 16
NOTE = SLOTS * R
AUX = 24
MSG = NOTE + AUX
NOTE_LANES = 2 * UNIT
PLACE = 2 * HALO
NOTE_AT = 2 * PLACE
COUNT_AT = 3 * PLACE
EDGE = 24
NT = (((1,), (1,)), ((), ()))
BF = jnp.bfloat16
F32 = jnp.float32


def dot(left, right, dims=(((1,), (0,)), ((), ()))):
    return lax.dot_general(left, right, dims, preferred_element_type=F32)


def iota(shape, dim):
    return lax.broadcasted_iota(jnp.int32, shape, dim)


def roll(value, shift):
    width = value.shape[1]
    return pltpu.roll(value, shift % width, 1) if shift % width else value


def toeplitz(row, rows, shift=LANES - HALO):
    row = roll(row, shift % 8)
    return pltpu.roll(jnp.broadcast_to(row, (rows, row.shape[1])), shift // 8 * 8, 1, stride=1, stride_axis=0)


def sin_pi(value):
    folded = jnp.where(value > 0.5, 1.0 - value, jnp.where(value < -0.5, -1.0 - value, value))
    angle = jnp.pi * folded
    square = angle * angle
    total = jnp.full_like(angle, -1.0 / 39916800.0)
    for term in (1.0 / 362880.0, -1.0 / 5040.0, 1.0 / 120.0, -1.0 / 6.0, 1.0):
        total = total * square + term
    return total * angle


def lanczos_weights(frac):
    shape = (8, frac.shape[1])
    shift = iota(shape, 0)
    offset = jnp.broadcast_to(frac, shape) - (shift - 2).astype(F32)
    sine = sin_pi(jnp.broadcast_to(frac, shape))
    sine = jnp.where(shift % 2 == 0, sine, -sine)
    weights = 3.0 * sine * sin_pi(offset * (1.0 / 3.0)) / (jnp.pi * jnp.pi * offset * offset)
    return weights.astype(BF).astype(F32)


def seat(o):
    return (o + 2) % 8 * 4 + (o // 8 + 1) % 4


def tile_kernel(
    coeff_hbm, weight_hbm, owner_hbm, block_hbm,
    tile_hbm, row_taps_hbm, col_taps_hbm, start_x_hbm, frac_x_hbm, start_y_hbm, frac_y_hbm,
    out_ref,
    coeff_ref, weight_ref, owner_ref, block_ref,
    tile_ref, row_taps_ref, col_taps_ref, start_x_ref, frac_x_ref, start_y_ref, frac_y_ref,
    sems, taps_ref, window_ref, matched_ref, source_ref, col_ref, count_ref,
):
    pairs = [
        (row_taps_hbm, row_taps_ref), (tile_hbm, tile_ref), (col_taps_hbm, col_taps_ref),
        (coeff_hbm, coeff_ref), (frac_x_hbm, frac_x_ref), (start_x_hbm, start_x_ref),
        (start_y_hbm, start_y_ref), (frac_y_hbm, frac_y_ref), (weight_hbm, weight_ref),
        (owner_hbm, owner_ref), (block_hbm, block_ref),
    ]
    copies = [pltpu.make_async_copy(src, dst, sems.at[n]) for n, (src, dst) in enumerate(pairs)]
    for copy in copies:
        copy.start()
    taps_ref[...] = jnp.zeros_like(taps_ref)
    peers = out_ref.shape[0]
    for o in range(peers):
        count_ref[o] = 0
    out_ref[...] = jnp.zeros_like(out_ref)
    for copy in copies:
        copy.wait()
    taps_ref[0:NB, 0:KW] = row_taps_ref[...].astype(F32)
    taps_ref[8:8 + NB, 0:KW] = col_taps_ref[...].astype(F32)
    row_band = jnp.concatenate([toeplitz(taps_ref[k:k + 1, :], LANES, 0) for k in range(NB)], axis=0).astype(BF)
    col_bands = [toeplitz(taps_ref[8 + k:9 + k, 0:LANES], R)[:, 0:R].astype(BF) for k in range(NB)]
    moved = roll(tile_ref[0].astype(F32), HALO)
    before = iota((R, LANES), 1) < HALO
    for s in range(SPT + 1):
        strip = moved[:, s % SPT * LANES:(s % SPT + 1) * LANES]
        if s % SPT == 0:
            strip = jnp.where(before == (s > 0), strip, 0.0)
        strip = strip.astype(BF)
        if s < SPT:
            window_ref[s * R:(s + 1) * R, 0:LANES] = strip
        if s > 0:
            window_ref[(s - 1) * R:s * R, LANES:] = strip
    group = 16
    width = group * LANES
    for g in range(SPT // group):
        rows = group * R
        window = window_ref[g * rows:(g + 1) * rows, :]
        across = dot(window, row_band, NT).astype(BF)
        column = iota((1, width), 1) + g * width
        x_coord = (2 * column - (W - 1)).astype(F32) / (W - 1)
        y_coord = (2 * iota((R, 1), 0) - (R - 1)).astype(F32) / (R - 1)
        matched = jnp.zeros((R, width), F32)
        for k in range(NB):
            term = jnp.concatenate(
                [across[j * R:(j + 1) * R, k * LANES:(k + 1) * LANES] for j in range(group)], axis=1
            )
            basis_term = dot(col_bands[k], term)
            coeff_map = coeff_ref[0, 0, k] + coeff_ref[1, 0, k] * x_coord + coeff_ref[2, 0, k] * y_coord
            matched = matched + coeff_map * basis_term
        matched_ref[:, g * width:(g + 1) * width] = matched.astype(BF).astype(F32)
    moved = roll(matched_ref[...], 2)
    for s in range(SPT):
        strip = moved[:, s * LANES:(s + 1) * LANES].astype(BF)
        source_ref[s * R:(s + 1) * R, 0:LANES] = strip
        before = (s - 1) % SPT
        source_ref[before * R:(before + 1) * R, LANES:] = strip
    weights_x = lanczos_weights(frac_x_ref[...])
    chunk = 512
    deep = LANES + 16
    order = iota((deep, chunk), 0).astype(F32).astype(BF)
    for c in range(W // chunk):
        cols = slice(c * chunk, (c + 1) * chunk)
        start = start_x_ref[:, cols]
        tap = order - (start % LANES).astype(F32).astype(BF)
        taps = jnp.zeros((deep, chunk), BF)
        for s in range(6):
            taps = jnp.where(tap == s, weights_x[s:s + 1, cols].astype(BF), taps)
        taps = jnp.concatenate([taps, jnp.zeros((2 * LANES - deep, chunk), BF)], axis=0)
        found = dot(source_ref[...], taps)
        place = jnp.broadcast_to(start // LANES, (8, chunk))
        total = found[0:R].reshape(R // 8, 8, chunk)
        for s in range(1, SPT):
            part = found[s * R:(s + 1) * R].reshape(R // 8, 8, chunk)
            total = jnp.where((place == s)[None], part, total)
        col_ref[:, cols] = total.reshape(R, chunk).astype(BF)
    weights_y = lanczos_weights(frac_y_ref[...])
    step = iota((R, R), 0) - start_y_ref[...]
    warp_y = jnp.zeros((R, R), F32)
    for s in range(6):
        warp_y = jnp.where(step == s - 2, weights_y[s:s + 1, :], warp_y)
    warped = dot(warp_y.T.astype(BF), col_ref[...]).astype(BF)
    weight = weight_ref[...].astype(F32)
    row = iota((AUX, LANES), 0)
    lane = iota((AUX, LANES), 1)
    place = lane - NOTE_AT
    last = row - (AUX - 8)
    noted = (last >= 0) & (place >= 0) & (place < NOTE_LANES)
    base = jnp.where(noted & (last == 2), weight, 0.0).astype(BF)
    for o in range(peers):
        out_ref[o, NOTE:MSG, :] = base

    def add(owner, piece):
        owner = seat(owner)
        out_ref[owner, NOTE:MSG, :] = (out_ref[owner, NOTE:MSG, :].astype(F32) + piece).astype(BF)

    def add_edges(owner, strip, lanes, side):
        strip = strip.astype(F32)
        units = []
        for t in range(AUX // 8):
            at = lane[0:8] - side * HALO
            unit = jnp.where(lane[0:8] == COUNT_AT + side, 1.0, 0.0)
            for f in range(3):
                n = 3 * t + f
                if n < R // 8:
                    part = roll(strip[n * 8:(n + 1) * 8], f * PLACE + side * HALO - lanes)
                    unit = jnp.where((at >= f * PLACE) & (at < f * PLACE + HALO), part, unit)
            units.append(unit)
        add(owner, jnp.concatenate(units, axis=0))

    for s in range(SPT):
        owner, block = owner_ref[0, s], block_ref[0, s]
        slot = count_ref[owner]
        count_ref[owner] = slot + 1
        strip = warped[:, s * LANES:(s + 1) * LANES]
        out_ref[seat(owner), pl.ds(pl.multiple_of(slot * R, R), R), :] = strip
        note = jnp.where(last == 0, weight, jnp.where(last == 1, block.astype(F32), 0.0))
        add(owner, jnp.where(noted & (place // UNIT == slot), note, 0.0))

        @pl.when((block == SPT - 1) | (block == 0))
        def _():
            pl.when((block > 0) & (owner < peers - 1))(
                lambda: add_edges(owner + 1, strip, LANES - HALO, 0)
            )
            pl.when((block == 0) & (owner > 0))(lambda: add_edges(owner - 1, strip, 0, 1))


def split(value):
    high = value.astype(BF)
    return high, (value - high.astype(F32)).astype(BF)


def taper_bands(width, rows, shift):
    lane = iota((1, width), 1)
    at = lane - HALO
    taps = jnp.where(lane < KW, 441 - at * at, 0).astype(F32)
    high, low = split(toeplitz(taps, rows, shift))
    return jnp.concatenate([high, low], axis=0)


def band_kernel(across_ref, down_ref):
    across_ref[...] = taper_bands(3 * LANES, LANES, LANES - HALO)
    down_ref[...] = taper_bands(LANES, R, EDGE - HALO)


def sum_kernel(in_ref, band_ref, coadd_ref, mid_ref, chip_ref, next_ref, stack_ref):
    peers = in_ref.shape[0]
    depth = peers * NOTE_LANES
    aux = [in_ref[v, NOTE:MSG, :].astype(F32) for v in range(peers)]
    notes = []
    per_row = LANES // NOTE_LANES
    lane = iota((8, LANES), 1)
    for q in range(peers // per_row):
        total = jnp.zeros((8, LANES), F32)
        for j in range(per_row):
            note = roll(aux[q * per_row + j][AUX - 8:], j * NOTE_LANES - NOTE_AT)
            total = jnp.where(lane // NOTE_LANES == j, note, total)
        notes.append(total)
    notes = jnp.concatenate(notes, axis=1)
    weight, block, peer_weight = notes[0:1], notes[1:2], notes[2:3]
    same = iota((UNIT, depth), 0) == iota((UNIT, depth), 1) % UNIT
    spread = jnp.concatenate(
        [jnp.where(same, jnp.where(block == b, weight, 0.0), 0.0) for b in range(SPT)], axis=0
    ).astype(BF)
    parts = []
    for g in range(R // UNIT):
        pieces = [
            in_ref[v, slot * R + g * UNIT:slot * R + (g + 1) * UNIT, :]
            for v in range(peers) for slot in range(SLOTS)
        ]
        parts.append(jnp.concatenate(pieces, axis=0))
    parts.append(jnp.ones((depth, LANES), BF))
    total = dot(spread, jnp.concatenate(parts, axis=1))
    scale = 1.0 / (total[:, R // UNIT * LANES:] + 1.0)
    for b in range(SPT):
        for g in range(R // UNIT):
            rows = slice(b * UNIT, (b + 1) * UNIT)
            value = total[rows, g * LANES:(g + 1) * LANES] * scale[rows]
            coadd_ref[g * UNIT:(g + 1) * UNIT, b * LANES:(b + 1) * LANES] = value
            stack_ref[(b + 1) * R + g * UNIT:(b + 1) * R + (g + 1) * UNIT, :] = value
    same = iota((AUX, depth), 0) == iota((AUX, depth), 1) % NOTE_LANES
    gap = jnp.zeros((NOTE_LANES - AUX, LANES), F32)
    edges = jnp.concatenate([x for v in range(peers) for x in (aux[v], gap)], axis=0).astype(BF)
    edges = dot(jnp.where(same, peer_weight, 0.0).astype(BF), edges)
    for side, block in enumerate((0, SPT + 1)):
        sum_weight = edges[AUX - 8:AUX - 7, COUNT_AT + side:COUNT_AT + side + 1]
        value = edges * (1.0 / (sum_weight + 1.0))
        for n in range(R // 8):
            t, f = n // 3, n % 3
            to = (LANES - HALO, 0)[side] - f * PLACE - side * HALO
            stack_ref[block * R + n * 8:block * R + n * 8 + 8, :] = roll(value[t * 8:t * 8 + 8], to)
    band = band_ref[...]
    high, low = split(stack_ref[...])
    window = jnp.concatenate(
        [
            jnp.concatenate([part[j * R:(j + SPT) * R] for j in range(3)], axis=1)
            for part in (high, low)
        ],
        axis=0,
    )
    mid = dot(window, band, NT)
    mid = (mid[0:SPT * R] + mid[SPT * R:])
    mid = mid[:, 0:LANES] + mid[:, LANES:]
    for s in range(SPT):
        mid_ref[:, s * LANES:(s + 1) * LANES] = mid[s * R:(s + 1) * R]
    even = lax.axis_index("sky") % 2 == 0
    first, last = mid_ref[0:EDGE, :], mid_ref[R - EDGE:R, :]
    chip_ref[...] = jnp.where(even, last, first).astype(BF)
    next_ref[...] = jnp.where(even, first, last).astype(BF)


def down_kernel(mid_ref, chip_ref, next_ref, band_ref, out_ref):
    norm = sum((1.0 - (a / 21.0) ** 2) ** 2 for a in range(-HALO, HALO + 1))
    even = lax.axis_index("sky") % 2 == 0
    chip, following = chip_ref[...].astype(F32), next_ref[...].astype(F32)
    above, below = jnp.where(even, following, chip), jnp.where(even, chip, following)
    rows = jnp.concatenate([above, mid_ref[...], below], axis=0)
    band = band_ref[:, 0:R + 2 * EDGE]
    high, low = split(rows)
    total = dot(jnp.concatenate([band, band], axis=1), jnp.concatenate([high, low], axis=0))
    out_ref[...] = (total[0:R] + total[R:]) * (1.0 / (441.0 * 441.0 * norm))


def vmem(n):
    return [pl.BlockSpec(memory_space=pltpu.VMEM)] * n


GRANT = 56 * 1024 * 1024
PARAMS = pltpu.CompilerParams(vmem_limit_bytes=40 * 1024 * 1024)


def tile_call(peers, *operands):
    spaces = [pltpu.SMEM, pltpu.VMEM, pltpu.SMEM, pltpu.SMEM] + [pltpu.VMEM] * 7
    return pl.pallas_call(
        tile_kernel,
        out_shape=jax.ShapeDtypeStruct((peers, MSG, LANES), BF),
        in_specs=[pl.BlockSpec(memory_space=pltpu.HBM)] * len(operands),
        out_specs=pl.BlockSpec(memory_space=pltpu.VMEM),
        scratch_shapes=[space(x.shape, x.dtype) for space, x in zip(spaces, operands)] + [
            pltpu.SemaphoreType.DMA((len(operands),)),
            pltpu.VMEM((16, 2 * LANES), F32),
            pltpu.VMEM((SPT * R, 2 * LANES), BF),
            pltpu.VMEM((R, W), F32),
            pltpu.VMEM((SPT * R, 2 * LANES), BF),
            pltpu.VMEM((R, W), BF),
            pltpu.SMEM((peers,), jnp.int32),
        ],
        compiler_params=pltpu.CompilerParams(vmem_limit_bytes=GRANT),
    )(*operands)


def sum_call(received, band):
    image = jax.ShapeDtypeStruct((R, W), F32)
    rows = jax.ShapeDtypeStruct((EDGE, W), BF)
    return pl.pallas_call(
        sum_kernel,
        out_shape=(image, image, rows, rows),
        in_specs=vmem(2),
        out_specs=tuple(vmem(4)),
        scratch_shapes=[pltpu.VMEM(((SPT + 2) * R, LANES), F32)],
        compiler_params=PARAMS,
    )(received, band)


def down_call(mid, from_chip, from_next, band):
    return pl.pallas_call(
        down_kernel,
        out_shape=jax.ShapeDtypeStruct((R, W), F32),
        in_specs=vmem(4),
        out_specs=pl.BlockSpec(memory_space=pltpu.VMEM),
        compiler_params=PARAMS,
    )(mid, from_chip, from_next, band)


def local(
    ccd_tiles, row_taps, col_taps, psf_coeffs, warp_start_x, warp_frac_x, warp_start_y, warp_frac_y,
    tile_weight, strip_owner, strip_block,
):
    peers = lax.axis_size("visit")
    operands = (
        psf_coeffs.transpose(2, 0, 1), tile_weight.reshape(1, 1), strip_owner.reshape(1, SPT), strip_block,
        ccd_tiles, row_taps, col_taps, warp_start_x, warp_frac_x, warp_start_y, warp_frac_y,
    )
    messages = tile_call(peers, *operands)
    band_across, band_down = pl.pallas_call(
        band_kernel,
        out_shape=(jax.ShapeDtypeStruct((2 * LANES, 3 * LANES), BF), jax.ShapeDtypeStruct((2 * R, LANES), BF)),
        out_specs=tuple(vmem(2)),
        compiler_params=PARAMS,
    )()
    groups = [sorted(range(peers), key=seat)]
    received = lax.all_to_all(messages, "visit", 0, 0, tiled=True, axis_index_groups=groups)
    coadd, mid, to_chip, to_next = sum_call(received, band_across)
    size = lax.axis_size("sky")
    swap = lambda first: [p for i in range(first, size - 1, 2) for p in ((i, i + 1), (i + 1, i))]
    from_next = lax.ppermute(to_next, "sky", swap(1))
    from_chip = lax.ppermute(to_chip, "sky", swap(0))
    detection = down_call(mid, from_chip, from_next, band_down)
    return coadd, detection


def solution(mesh):
    tiles = ("visit", "sky")
    in_specs = (
        P(tiles, None, None),
        P(),
        P(),
        P(tiles, None, None),
        P(tiles, None),
        P(tiles, None),
        P(tiles, None),
        P(tiles, None),
        P(tiles),
        P(tiles, None, None),
        P(tiles, None),
    )
    out_specs = (P("sky", "visit"), P("sky", "visit"))
    return jax.shard_map(local, mesh=mesh, in_specs=in_specs, out_specs=out_specs, check_vma=False)
```

```python
import jax
import jax.numpy as jnp
from jax import lax
from jax.experimental import pallas as pl
from jax.experimental.pallas import tpu as pltpu
from jax.sharding import PartitionSpec as P

R = 64
W = 2048
NB = 5
KW = 41
HALO = 20
SPT = 16
SPAN = 240
WINDOWS = -(-W // SPAN)
SLOTS = 2
LANES = 128
UNIT = 16
NOTE = SLOTS * R
AUX = 24
MSG = NOTE + AUX
NOTE_LANES = 2 * UNIT
PLACE = 2 * HALO
NOTE_AT = 2 * PLACE
COUNT_AT = 3 * PLACE
EDGE = 24
NT = (((1,), (1,)), ((), ()))
BF = jnp.bfloat16
F32 = jnp.float32


def dot(left, right, dims=(((1,), (0,)), ((), ()))):
    return lax.dot_general(left, right, dims, preferred_element_type=F32)


def iota(shape, dim):
    return lax.broadcasted_iota(jnp.int32, shape, dim)


def roll(value, shift):
    width = value.shape[1]
    return pltpu.roll(value, shift % width, 1) if shift % width else value


def toeplitz(row, rows, shift=LANES - HALO):
    row = roll(row, shift % 8)
    return pltpu.roll(jnp.broadcast_to(row, (rows, row.shape[1])), shift // 8 * 8, 1, stride=1, stride_axis=0)


def sin_pi(value):
    folded = jnp.where(value > 0.5, 1.0 - value, jnp.where(value < -0.5, -1.0 - value, value))
    angle = jnp.pi * folded
    square = angle * angle
    total = jnp.full_like(angle, -1.0 / 39916800.0)
    for term in (1.0 / 362880.0, -1.0 / 5040.0, 1.0 / 120.0, -1.0 / 6.0, 1.0):
        total = total * square + term
    return total * angle


def lanczos_weights(frac):
    shape = (8, frac.shape[1])
    shift = iota(shape, 0)
    offset = jnp.broadcast_to(frac, shape) - (shift - 2).astype(F32)
    sine = sin_pi(jnp.broadcast_to(frac, shape))
    sine = jnp.where(shift % 2 == 0, sine, -sine)
    weights = 3.0 * sine * sin_pi(offset * (1.0 / 3.0)) / (jnp.pi * jnp.pi * offset * offset)
    return weights.astype(BF).astype(F32)


def seat(o):
    return (o + 2) % 8 * 4 + (o // 8 + 1) % 4


def tile_kernel(
    coeff_hbm, weight_hbm, owner_hbm, block_hbm,
    tile_hbm, row_taps_hbm, col_taps_hbm, start_x_hbm, frac_x_hbm, start_y_hbm, frac_y_hbm,
    out_ref,
    coeff_ref, weight_ref, owner_ref, block_ref,
    tile_ref, row_taps_ref, col_taps_ref, start_x_ref, frac_x_ref, start_y_ref, frac_y_ref,
    sems, taps_ref, window_ref, matched_ref, source_ref, col_ref, count_ref,
):
    pairs = [
        (row_taps_hbm, row_taps_ref), (tile_hbm, tile_ref), (col_taps_hbm, col_taps_ref),
        (coeff_hbm, coeff_ref), (frac_x_hbm, frac_x_ref), (start_x_hbm, start_x_ref),
        (start_y_hbm, start_y_ref), (frac_y_hbm, frac_y_ref), (weight_hbm, weight_ref),
        (owner_hbm, owner_ref), (block_hbm, block_ref),
    ]
    copies = [pltpu.make_async_copy(src, dst, sems.at[n]) for n, (src, dst) in enumerate(pairs)]
    for copy in copies:
        copy.start()
    taps_ref[...] = jnp.zeros_like(taps_ref)
    peers = out_ref.shape[0]
    for o in range(peers):
        count_ref[o] = 0
    out_ref[...] = jnp.zeros_like(out_ref)
    for copy in copies:
        copy.wait()
    taps_ref[0:NB, 0:KW] = row_taps_ref[...].astype(F32)
    taps_ref[8:8 + NB, 0:KW] = col_taps_ref[...].astype(F32)
    row_band = jnp.concatenate([toeplitz(taps_ref[k:k + 1, :], LANES, 0) for k in range(NB)], axis=0).astype(BF)
    col_bands = [toeplitz(taps_ref[8 + k:9 + k, 0:LANES], R)[:, 0:R].astype(BF) for k in range(NB)]
    moved = roll(tile_ref[0].astype(F32), HALO)
    before = iota((R, LANES), 1) < HALO
    for s in range(SPT + 1):
        strip = moved[:, s % SPT * LANES:(s % SPT + 1) * LANES]
        if s % SPT == 0:
            strip = jnp.where(before == (s > 0), strip, 0.0)
        strip = strip.astype(BF)
        if s < SPT:
            window_ref[s * R:(s + 1) * R, 0:LANES] = strip
        if s > 0:
            window_ref[(s - 1) * R:s * R, LANES:] = strip
    group = 16
    width = group * LANES
    for g in range(SPT // group):
        rows = group * R
        window = window_ref[g * rows:(g + 1) * rows, :]
        across = dot(window, row_band, NT).astype(BF)
        column = iota((1, width), 1) + g * width
        x_coord = (2 * column - (W - 1)).astype(F32) / (W - 1)
        y_coord = (2 * iota((R, 1), 0) - (R - 1)).astype(F32) / (R - 1)
        matched = jnp.zeros((R, width), F32)
        for k in range(NB):
            term = jnp.concatenate(
                [across[j * R:(j + 1) * R, k * LANES:(k + 1) * LANES] for j in range(group)], axis=1
            )
            basis_term = dot(col_bands[k], term)
            coeff_map = coeff_ref[0, 0, k] + coeff_ref[1, 0, k] * x_coord + coeff_ref[2, 0, k] * y_coord
            matched = matched + coeff_map * basis_term
        matched_ref[:, g * width:(g + 1) * width] = matched.astype(BF).astype(F32)
    for n in range(WINDOWS):
        first = n * SPAN - 2
        blocks = [(first // LANES + j) % SPT * LANES for j in range(3)]
        region = jnp.concatenate([matched_ref[:, at:at + LANES] for at in blocks], axis=1)
        source_ref[n * R:(n + 1) * R, :] = roll(region, -(first % LANES))[:, 0:2 * LANES].astype(BF)
    weights_x = lanczos_weights(frac_x_ref[...])
    chunk = 1024
    order = iota((2 * LANES, chunk), 0).astype(F32).astype(BF)
    for c in range(W // chunk):
        cols = slice(c * chunk, (c + 1) * chunk)
        start = start_x_ref[:, cols]
        place = ((start.astype(F32) + 0.5) * (1.0 / SPAN)).astype(jnp.int32)
        tap = order - (start - place * SPAN).astype(F32).astype(BF)
        taps = jnp.zeros((2 * LANES, chunk), BF)
        for s in range(6):
            taps = jnp.where(tap == s, weights_x[s:s + 1, cols].astype(BF), taps)
        found = dot(source_ref[...], taps)
        place = jnp.broadcast_to(place, (8, chunk))
        total = found[0:R].reshape(R // 8, 8, chunk)
        for s in range(1, WINDOWS):
            part = found[s * R:(s + 1) * R].reshape(R // 8, 8, chunk)
            total = jnp.where((place == s)[None], part, total)
        col_ref[:, cols] = total.reshape(R, chunk).astype(BF)
    weights_y = lanczos_weights(frac_y_ref[...])
    step = iota((R, R), 0) - start_y_ref[...]
    warp_y = jnp.zeros((R, R), F32)
    for s in range(6):
        warp_y = jnp.where(step == s - 2, weights_y[s:s + 1, :], warp_y)
    warped = dot(warp_y.T.astype(BF), col_ref[...]).astype(BF)
    weight = weight_ref[...].astype(F32)
    row = iota((AUX, LANES), 0)
    lane = iota((AUX, LANES), 1)
    place = lane - NOTE_AT
    last = row - (AUX - 8)
    noted = (last >= 0) & (place >= 0) & (place < NOTE_LANES)
    base = jnp.where(noted & (last == 2), weight, 0.0).astype(BF)
    for o in range(peers):
        out_ref[o, NOTE:MSG, :] = base

    def add(owner, piece):
        owner = seat(owner)
        out_ref[owner, NOTE:MSG, :] = (out_ref[owner, NOTE:MSG, :].astype(F32) + piece).astype(BF)

    def add_edges(owner, strip, lanes, side):
        strip = strip.astype(F32)
        units = []
        for t in range(AUX // 8):
            at = lane[0:8] - side * HALO
            unit = jnp.where(lane[0:8] == COUNT_AT + side, 1.0, 0.0)
            for f in range(3):
                n = 3 * t + f
                if n < R // 8:
                    part = roll(strip[n * 8:(n + 1) * 8], f * PLACE + side * HALO - lanes)
                    unit = jnp.where((at >= f * PLACE) & (at < f * PLACE + HALO), part, unit)
            units.append(unit)
        add(owner, jnp.concatenate(units, axis=0))

    for s in range(SPT):
        owner, block = owner_ref[0, s], block_ref[0, s]
        slot = count_ref[owner]
        count_ref[owner] = slot + 1
        strip = warped[:, s * LANES:(s + 1) * LANES]
        out_ref[seat(owner), pl.ds(pl.multiple_of(slot * R, R), R), :] = strip
        note = jnp.where(last == 0, weight, jnp.where(last == 1, block.astype(F32), 0.0))
        add(owner, jnp.where(noted & (place // UNIT == slot), note, 0.0))

        @pl.when((block == SPT - 1) | (block == 0))
        def _():
            pl.when((block > 0) & (owner < peers - 1))(
                lambda: add_edges(owner + 1, strip, LANES - HALO, 0)
            )
            pl.when((block == 0) & (owner > 0))(lambda: add_edges(owner - 1, strip, 0, 1))


def split(value):
    high = value.astype(BF)
    return high, (value - high.astype(F32)).astype(BF)


def taper_bands(width, rows, shift):
    lane = iota((1, width), 1)
    at = lane - HALO
    taps = jnp.where(lane < KW, 441 - at * at, 0).astype(F32)
    high, low = split(toeplitz(taps, rows, shift))
    return jnp.concatenate([high, low], axis=0)


def band_kernel(across_ref, down_ref):
    across_ref[...] = taper_bands(2 * LANES, LANES, 0)
    down_ref[...] = taper_bands(LANES, R, EDGE - HALO)


def sum_kernel(in_ref, band_ref, coadd_ref, mid_ref, chip_ref, next_ref, stack_ref):
    peers = in_ref.shape[0]
    depth = peers * NOTE_LANES
    aux = [in_ref[v, NOTE:MSG, :].astype(F32) for v in range(peers)]
    notes = []
    per_row = LANES // NOTE_LANES
    lane = iota((8, LANES), 1)
    for q in range(peers // per_row):
        total = jnp.zeros((8, LANES), F32)
        for j in range(per_row):
            note = roll(aux[q * per_row + j][AUX - 8:], j * NOTE_LANES - NOTE_AT)
            total = jnp.where(lane // NOTE_LANES == j, note, total)
        notes.append(total)
    notes = jnp.concatenate(notes, axis=1)
    weight, block, peer_weight = notes[0:1], notes[1:2], notes[2:3]
    same = iota((UNIT, depth), 0) == iota((UNIT, depth), 1) % UNIT
    spread = jnp.concatenate(
        [jnp.where(same, jnp.where(block == b, weight, 0.0), 0.0) for b in range(SPT)], axis=0
    ).astype(BF)
    parts = []
    for g in range(R // UNIT):
        pieces = [
            in_ref[v, slot * R + g * UNIT:slot * R + (g + 1) * UNIT, :]
            for v in range(peers) for slot in range(SLOTS)
        ]
        parts.append(jnp.concatenate(pieces, axis=0))
    parts.append(jnp.ones((depth, LANES), BF))
    total = dot(spread, jnp.concatenate(parts, axis=1))
    scale = 1.0 / (total[:, R // UNIT * LANES:] + 1.0)
    for b in range(SPT):
        for g in range(R // UNIT):
            rows = slice(b * UNIT, (b + 1) * UNIT)
            value = total[rows, g * LANES:(g + 1) * LANES] * scale[rows]
            coadd_ref[g * UNIT:(g + 1) * UNIT, b * LANES:(b + 1) * LANES] = value
            stack_ref[(b + 1) * R + g * UNIT:(b + 1) * R + (g + 1) * UNIT, :] = value
    same = iota((AUX, depth), 0) == iota((AUX, depth), 1) % NOTE_LANES
    gap = jnp.zeros((NOTE_LANES - AUX, LANES), F32)
    edges = jnp.concatenate([x for v in range(peers) for x in (aux[v], gap)], axis=0).astype(BF)
    edges = dot(jnp.where(same, peer_weight, 0.0).astype(BF), edges)
    for side, block in enumerate((0, SPT + 1)):
        sum_weight = edges[AUX - 8:AUX - 7, COUNT_AT + side:COUNT_AT + side + 1]
        value = edges * (1.0 / (sum_weight + 1.0))
        for n in range(R // 8):
            t, f = n // 3, n % 3
            to = (LANES - HALO, 0)[side] - f * PLACE - side * HALO
            stack_ref[block * R + n * 8:block * R + n * 8 + 8, :] = roll(value[t * 8:t * 8 + 8], to)
    band = band_ref[...]
    moved = roll(stack_ref[...], HALO)
    strips = (SPT + 1) * R
    moved = jnp.where(iota((strips, LANES), 1) < HALO, moved[0:strips], moved[R:])
    window = jnp.concatenate(
        [jnp.concatenate([part[0:SPT * R], part[R:]], axis=1) for part in split(moved)], axis=0
    )
    mid = dot(window, band, NT)
    mid = (mid[0:SPT * R] + mid[SPT * R:])
    mid = mid[:, 0:LANES] + mid[:, LANES:]
    for s in range(SPT):
        mid_ref[:, s * LANES:(s + 1) * LANES] = mid[s * R:(s + 1) * R]
    even = lax.axis_index("sky") % 2 == 0
    first, last = mid_ref[0:EDGE, :], mid_ref[R - EDGE:R, :]
    chip_ref[...] = jnp.where(even, last, first).astype(BF)
    next_ref[...] = jnp.where(even, first, last).astype(BF)


def down_kernel(mid_ref, chip_ref, next_ref, band_ref, out_ref):
    norm = sum((1.0 - (a / 21.0) ** 2) ** 2 for a in range(-HALO, HALO + 1))
    even = lax.axis_index("sky") % 2 == 0
    chip, following = chip_ref[...].astype(F32), next_ref[...].astype(F32)
    above, below = jnp.where(even, following, chip), jnp.where(even, chip, following)
    rows = jnp.concatenate([above, mid_ref[...], below], axis=0)
    band = band_ref[:, 0:R + 2 * EDGE]
    high, low = split(rows)
    total = dot(jnp.concatenate([band, band], axis=1), jnp.concatenate([high, low], axis=0))
    out_ref[...] = (total[0:R] + total[R:]) * (1.0 / (441.0 * 441.0 * norm))


def vmem(n):
    return [pl.BlockSpec(memory_space=pltpu.VMEM)] * n


GRANT = 56 * 1024 * 1024
PARAMS = pltpu.CompilerParams(vmem_limit_bytes=40 * 1024 * 1024)


def tile_call(peers, *operands):
    spaces = [pltpu.SMEM, pltpu.VMEM, pltpu.SMEM, pltpu.SMEM] + [pltpu.VMEM] * 7
    return pl.pallas_call(
        tile_kernel,
        out_shape=jax.ShapeDtypeStruct((peers, MSG, LANES), BF),
        in_specs=[pl.BlockSpec(memory_space=pltpu.HBM)] * len(operands),
        out_specs=pl.BlockSpec(memory_space=pltpu.VMEM),
        scratch_shapes=[space(x.shape, x.dtype) for space, x in zip(spaces, operands)] + [
            pltpu.SemaphoreType.DMA((len(operands),)),
            pltpu.VMEM((16, 2 * LANES), F32),
            pltpu.VMEM((SPT * R, 2 * LANES), BF),
            pltpu.VMEM((R, W), F32),
            pltpu.VMEM((WINDOWS * R, 2 * LANES), BF),
            pltpu.VMEM((R, W), BF),
            pltpu.SMEM((peers,), jnp.int32),
        ],
        compiler_params=pltpu.CompilerParams(vmem_limit_bytes=GRANT),
    )(*operands)


def sum_call(received, band):
    image = jax.ShapeDtypeStruct((R, W), F32)
    rows = jax.ShapeDtypeStruct((EDGE, W), BF)
    return pl.pallas_call(
        sum_kernel,
        out_shape=(image, image, rows, rows),
        in_specs=vmem(2),
        out_specs=tuple(vmem(4)),
        scratch_shapes=[pltpu.VMEM(((SPT + 2) * R, LANES), F32)],
        compiler_params=PARAMS,
    )(received, band)


def down_call(mid, from_chip, from_next, band):
    return pl.pallas_call(
        down_kernel,
        out_shape=jax.ShapeDtypeStruct((R, W), F32),
        in_specs=vmem(4),
        out_specs=pl.BlockSpec(memory_space=pltpu.VMEM),
        compiler_params=PARAMS,
    )(mid, from_chip, from_next, band)


def local(
    ccd_tiles, row_taps, col_taps, psf_coeffs, warp_start_x, warp_frac_x, warp_start_y, warp_frac_y,
    tile_weight, strip_owner, strip_block,
):
    peers = lax.axis_size("visit")
    operands = (
        psf_coeffs.transpose(2, 0, 1), tile_weight.reshape(1, 1), strip_owner.reshape(1, SPT), strip_block,
        ccd_tiles, row_taps, col_taps, warp_start_x, warp_frac_x, warp_start_y, warp_frac_y,
    )
    messages = tile_call(peers, *operands)
    band_across, band_down = pl.pallas_call(
        band_kernel,
        out_shape=(jax.ShapeDtypeStruct((2 * LANES, 2 * LANES), BF), jax.ShapeDtypeStruct((2 * R, LANES), BF)),
        out_specs=tuple(vmem(2)),
        compiler_params=PARAMS,
    )()
    groups = [sorted(range(peers), key=seat)]
    received = lax.all_to_all(messages, "visit", 0, 0, tiled=True, axis_index_groups=groups)
    coadd, mid, to_chip, to_next = sum_call(received, band_across)
    size = lax.axis_size("sky")
    swap = lambda first: [p for i in range(first, size - 1, 2) for p in ((i, i + 1), (i + 1, i))]
    from_next = lax.ppermute(to_next, "sky", swap(1))
    from_chip = lax.ppermute(to_chip, "sky", swap(0))
    detection = down_call(mid, from_chip, from_next, band_down)
    return coadd, detection


def solution(mesh):
    tiles = ("visit", "sky")
    in_specs = (
        P(tiles, None, None),
        P(),
        P(),
        P(tiles, None, None),
        P(tiles, None),
        P(tiles, None),
        P(tiles, None),
        P(tiles, None),
        P(tiles),
        P(tiles, None, None),
        P(tiles, None),
    )
    out_specs = (P("sky", "visit"), P("sky", "visit"))
    return jax.shard_map(local, mesh=mesh, in_specs=in_specs, out_specs=out_specs, check_vma=False)
```

```python
import jax
import jax.numpy as jnp
from jax import lax
from jax.experimental import pallas as pl
from jax.experimental.pallas import tpu as pltpu
from jax.sharding import PartitionSpec as P

R = 64
W = 2048
NB = 5
KW = 41
HALO = 20
SPT = 16
SPAN = 240
WINDOWS = -(-W // SPAN)
SLOTS = 2
LANES = 128
UNIT = 16
NOTE = SLOTS * R
AUX = 24
MSG = NOTE + AUX
NOTE_LANES = 2 * UNIT
PLACE = 2 * HALO
NOTE_AT = 2 * PLACE
COUNT_AT = 3 * PLACE
EDGE = 24
NT = (((1,), (1,)), ((), ()))
BF = jnp.bfloat16
F32 = jnp.float32


def dot(left, right, dims=(((1,), (0,)), ((), ()))):
    return lax.dot_general(left, right, dims, preferred_element_type=F32)


def iota(shape, dim):
    return lax.broadcasted_iota(jnp.int32, shape, dim)


def roll(value, shift):
    width = value.shape[1]
    return pltpu.roll(value, shift % width, 1) if shift % width else value


def toeplitz(row, rows, shift=LANES - HALO):
    row = roll(row, shift % 8)
    return pltpu.roll(jnp.broadcast_to(row, (rows, row.shape[1])), shift // 8 * 8, 1, stride=1, stride_axis=0)


def sin_pi(value):
    folded = jnp.where(value > 0.5, 1.0 - value, jnp.where(value < -0.5, -1.0 - value, value))
    angle = jnp.pi * folded
    square = angle * angle
    total = jnp.full_like(angle, -1.0 / 39916800.0)
    for term in (1.0 / 362880.0, -1.0 / 5040.0, 1.0 / 120.0, -1.0 / 6.0, 1.0):
        total = total * square + term
    return total * angle


def lanczos_weights(frac):
    shape = (8, frac.shape[1])
    shift = iota(shape, 0)
    offset = jnp.broadcast_to(frac, shape) - (shift - 2).astype(F32)
    sine = sin_pi(jnp.broadcast_to(frac, shape))
    sine = jnp.where(shift % 2 == 0, sine, -sine)
    weights = 3.0 * sine * sin_pi(offset * (1.0 / 3.0)) / (jnp.pi * jnp.pi * offset * offset)
    return weights.astype(BF).astype(F32)


def seat(o):
    return (o + 2) % 8 * 4 + (o // 8 + 1) % 4


def tile_kernel(
    coeff_hbm, weight_hbm, owner_hbm, block_hbm,
    tile_hbm, row_taps_hbm, col_taps_hbm, start_x_hbm, frac_x_hbm, start_y_hbm, frac_y_hbm,
    out_ref,
    coeff_ref, weight_ref, owner_ref, block_ref,
    tile_ref, row_taps_ref, col_taps_ref, start_x_ref, frac_x_ref, start_y_ref, frac_y_ref,
    sems, taps_ref, window_ref, matched_ref, source_ref, col_ref, count_ref,
):
    pairs = [
        (row_taps_hbm, row_taps_ref), (tile_hbm, tile_ref), (col_taps_hbm, col_taps_ref),
        (coeff_hbm, coeff_ref), (frac_x_hbm, frac_x_ref), (start_x_hbm, start_x_ref),
        (start_y_hbm, start_y_ref), (frac_y_hbm, frac_y_ref), (weight_hbm, weight_ref),
        (owner_hbm, owner_ref), (block_hbm, block_ref),
    ]
    copies = [pltpu.make_async_copy(src, dst, sems.at[n]) for n, (src, dst) in enumerate(pairs)]
    for copy in copies:
        copy.start()
    taps_ref[...] = jnp.zeros_like(taps_ref)
    peers = out_ref.shape[0]
    for o in range(peers):
        count_ref[o] = 0
    out_ref[...] = jnp.zeros_like(out_ref)
    for copy in copies:
        copy.wait()
    taps_ref[0:NB, 0:KW] = row_taps_ref[...].astype(F32)
    taps_ref[8:8 + NB, 0:KW] = col_taps_ref[...].astype(F32)
    row_band = jnp.concatenate([toeplitz(taps_ref[k:k + 1, :], LANES, 0) for k in range(NB)], axis=0).astype(BF)
    col_bands = [toeplitz(taps_ref[8 + k:9 + k, 0:LANES], R)[:, 0:R].astype(BF) for k in range(NB)]
    empty = jnp.zeros((R, R), BF)
    moved = roll(tile_ref[0].astype(F32), HALO)
    before = iota((R, LANES), 1) < HALO
    for s in range(SPT + 1):
        strip = moved[:, s % SPT * LANES:(s % SPT + 1) * LANES]
        if s % SPT == 0:
            strip = jnp.where(before == (s > 0), strip, 0.0)
        strip = strip.astype(BF)
        if s < SPT:
            window_ref[s * R:(s + 1) * R, 0:LANES] = strip
        if s > 0:
            window_ref[(s - 1) * R:s * R, LANES:] = strip
    group = 16
    width = group * LANES
    for g in range(SPT // group):
        rows = group * R
        window = window_ref[g * rows:(g + 1) * rows, :]
        across = dot(window, row_band, NT).astype(BF)
        column = iota((1, width), 1) + g * width
        x_coord = (2 * column - (W - 1)).astype(F32) / (W - 1)
        y_coord = (2 * iota((R, 1), 0) - (R - 1)).astype(F32) / (R - 1)
        terms = [
            jnp.concatenate(
                [across[j * R:(j + 1) * R, k * LANES:(k + 1) * LANES] for j in range(group)], axis=1
            )
            for k in range(NB)
        ]
        basis_terms = []
        for first in range(0, NB, 4):
            count = min(4, NB - first)
            bands = [
                jnp.concatenate([col_bands[first + k] if k == j else empty for j in range(count)], axis=1)
                for k in range(count)
            ]
            found = dot(jnp.concatenate(bands, axis=0), jnp.concatenate(terms[first:first + count], axis=0))
            basis_terms += [found[k * R:(k + 1) * R] for k in range(count)]
        matched = jnp.zeros((R, width), F32)
        for k in range(NB):
            coeff_map = coeff_ref[0, 0, k] + coeff_ref[1, 0, k] * x_coord + coeff_ref[2, 0, k] * y_coord
            matched = matched + coeff_map * basis_terms[k]
        matched_ref[:, g * width:(g + 1) * width] = matched.astype(BF).astype(F32)
    for n in range(WINDOWS):
        first = n * SPAN - 2
        blocks = [(first // LANES + j) % SPT * LANES for j in range(3)]
        region = jnp.concatenate([matched_ref[:, at:at + LANES] for at in blocks], axis=1)
        source_ref[n * R:(n + 1) * R, :] = roll(region, -(first % LANES))[:, 0:2 * LANES].astype(BF)
    weights_x = lanczos_weights(frac_x_ref[...])
    chunk = 1024
    order = iota((2 * LANES, chunk), 0).astype(F32).astype(BF)
    for c in range(W // chunk):
        cols = slice(c * chunk, (c + 1) * chunk)
        start = start_x_ref[:, cols]
        place = ((start.astype(F32) + 0.5) * (1.0 / SPAN)).astype(jnp.int32)
        tap = order - (start - place * SPAN).astype(F32).astype(BF)
        taps = jnp.zeros((2 * LANES, chunk), BF)
        for s in range(6):
            taps = jnp.where(tap == s, weights_x[s:s + 1, cols].astype(BF), taps)
        found = dot(source_ref[...], taps)
        place = jnp.broadcast_to(place, (8, chunk))
        total = found[0:R].reshape(R // 8, 8, chunk)
        for s in range(1, WINDOWS):
            part = found[s * R:(s + 1) * R].reshape(R // 8, 8, chunk)
            total = jnp.where((place == s)[None], part, total)
        col_ref[:, cols] = total.reshape(R, chunk).astype(BF)
    weights_y = lanczos_weights(frac_y_ref[...])
    step = iota((R, R), 0) - start_y_ref[...]
    warp_y = jnp.zeros((R, R), F32)
    for s in range(6):
        warp_y = jnp.where(step == s - 2, weights_y[s:s + 1, :], warp_y)
    warped = dot(warp_y.T.astype(BF), col_ref[...]).astype(BF)
    weight = weight_ref[...].astype(F32)
    row = iota((AUX, LANES), 0)
    lane = iota((AUX, LANES), 1)
    place = lane - NOTE_AT
    last = row - (AUX - 8)
    noted = (last >= 0) & (place >= 0) & (place < NOTE_LANES)
    base = jnp.where(noted & (last == 2), weight, 0.0).astype(BF)
    for o in range(peers):
        out_ref[o, NOTE:MSG, :] = base

    def add(owner, piece):
        owner = seat(owner)
        out_ref[owner, NOTE:MSG, :] = (out_ref[owner, NOTE:MSG, :].astype(F32) + piece).astype(BF)

    def add_edges(owner, strip, lanes, side):
        strip = strip.astype(F32)
        units = []
        for t in range(AUX // 8):
            at = lane[0:8] - side * HALO
            unit = jnp.where(lane[0:8] == COUNT_AT + side, 1.0, 0.0)
            for f in range(3):
                n = 3 * t + f
                if n < R // 8:
                    part = roll(strip[n * 8:(n + 1) * 8], f * PLACE + side * HALO - lanes)
                    unit = jnp.where((at >= f * PLACE) & (at < f * PLACE + HALO), part, unit)
            units.append(unit)
        add(owner, jnp.concatenate(units, axis=0))

    for s in range(SPT):
        owner, block = owner_ref[0, s], block_ref[0, s]
        slot = count_ref[owner]
        count_ref[owner] = slot + 1
        strip = warped[:, s * LANES:(s + 1) * LANES]
        out_ref[seat(owner), pl.ds(pl.multiple_of(slot * R, R), R), :] = strip
        note = jnp.where(last == 0, weight, jnp.where(last == 1, block.astype(F32), 0.0))
        add(owner, jnp.where(noted & (place // UNIT == slot), note, 0.0))

        @pl.when((block == SPT - 1) | (block == 0))
        def _():
            pl.when((block > 0) & (owner < peers - 1))(
                lambda: add_edges(owner + 1, strip, LANES - HALO, 0)
            )
            pl.when((block == 0) & (owner > 0))(lambda: add_edges(owner - 1, strip, 0, 1))


def split(value):
    high = value.astype(BF)
    return high, (value - high.astype(F32)).astype(BF)


def taper_bands(width, rows, shift):
    lane = iota((1, width), 1)
    at = lane - HALO
    taps = jnp.where(lane < KW, 441 - at * at, 0).astype(F32)
    high, low = split(toeplitz(taps, rows, shift))
    return jnp.concatenate([high, low], axis=0)


def band_kernel(across_ref, own_ref, halo_ref):
    across_ref[...] = taper_bands(2 * LANES, LANES, 0)
    own_ref[...] = taper_bands(LANES, R, LANES - HALO)
    band = taper_bands(LANES, R, EDGE - HALO).astype(F32)
    halo_ref[...] = jnp.where(iota(band.shape, 1) < EDGE, band, roll(band, -R)).astype(BF)


def sum_kernel(in_ref, band_ref, coadd_hbm, mid_ref, chip_ref, next_ref, stack_ref, coadd_ref, sem):
    peers = in_ref.shape[0]
    depth = peers * NOTE_LANES
    aux = [in_ref[v, NOTE:MSG, :].astype(F32) for v in range(peers)]
    notes = []
    per_row = LANES // NOTE_LANES
    lane = iota((8, LANES), 1)
    for q in range(peers // per_row):
        total = jnp.zeros((8, LANES), F32)
        for j in range(per_row):
            note = roll(aux[q * per_row + j][AUX - 8:], j * NOTE_LANES - NOTE_AT)
            total = jnp.where(lane // NOTE_LANES == j, note, total)
        notes.append(total)
    notes = jnp.concatenate(notes, axis=1)
    weight, block, peer_weight = notes[0:1], notes[1:2], notes[2:3]
    same = iota((UNIT, depth), 0) == iota((UNIT, depth), 1) % UNIT
    spread = jnp.concatenate(
        [jnp.where(same, jnp.where(block == b, weight, 0.0), 0.0) for b in range(SPT)], axis=0
    ).astype(BF)
    parts = []
    for g in range(R // UNIT):
        pieces = [
            in_ref[v, slot * R + g * UNIT:slot * R + (g + 1) * UNIT, :]
            for v in range(peers) for slot in range(SLOTS)
        ]
        parts.append(jnp.concatenate(pieces, axis=0))
    parts.append(jnp.ones((depth, LANES), BF))
    total = dot(spread, jnp.concatenate(parts, axis=1))
    scale = 1.0 / (total[:, R // UNIT * LANES:] + 1.0)
    for b in range(SPT):
        for g in range(R // UNIT):
            rows = slice(b * UNIT, (b + 1) * UNIT)
            value = total[rows, g * LANES:(g + 1) * LANES] * scale[rows]
            coadd_ref[g * UNIT:(g + 1) * UNIT, b * LANES:(b + 1) * LANES] = value
            stack_ref[(b + 1) * R + g * UNIT:(b + 1) * R + (g + 1) * UNIT, :] = value
    copy = pltpu.make_async_copy(coadd_ref, coadd_hbm, sem)
    copy.start()
    same = iota((AUX, depth), 0) == iota((AUX, depth), 1) % NOTE_LANES
    gap = jnp.zeros((NOTE_LANES - AUX, LANES), F32)
    edges = jnp.concatenate([x for v in range(peers) for x in (aux[v], gap)], axis=0).astype(BF)
    edges = dot(jnp.where(same, peer_weight, 0.0).astype(BF), edges)
    for side, block in enumerate((0, SPT + 1)):
        sum_weight = edges[AUX - 8:AUX - 7, COUNT_AT + side:COUNT_AT + side + 1]
        value = edges * (1.0 / (sum_weight + 1.0))
        for n in range(R // 8):
            t, f = n // 3, n % 3
            to = (LANES - HALO, 0)[side] - f * PLACE - side * HALO
            stack_ref[block * R + n * 8:block * R + n * 8 + 8, :] = roll(value[t * 8:t * 8 + 8], to)
    band = band_ref[...]
    moved = roll(stack_ref[...], HALO)
    strips = (SPT + 1) * R
    moved = jnp.where(iota((strips, LANES), 1) < HALO, moved[0:strips], moved[R:])
    window = jnp.concatenate(
        [jnp.concatenate([part[0:SPT * R], part[R:]], axis=1) for part in split(moved)], axis=0
    )
    mid = dot(window, band, NT)
    mid = (mid[0:SPT * R] + mid[SPT * R:])
    mid = mid[:, 0:LANES] + mid[:, LANES:]
    for s in range(SPT):
        mid_ref[:, s * LANES:(s + 1) * LANES] = mid[s * R:(s + 1) * R]
    even = lax.axis_index("sky") % 2 == 0
    first, last = mid_ref[0:EDGE, :], mid_ref[R - EDGE:R, :]
    chip_ref[...] = jnp.where(even, last, first).astype(BF)
    next_ref[...] = jnp.where(even, first, last).astype(BF)
    copy.wait()


SCALE = 1.0 / (441.0 * 441.0 * sum((1.0 - (a / 21.0) ** 2) ** 2 for a in range(-HALO, HALO + 1)))


def own_kernel(mid_ref, band_ref, out_ref):
    band = band_ref[:, 0:R]
    high, low = split(mid_ref[...])
    total = dot(jnp.concatenate([band, band], axis=1), jnp.concatenate([high, low], axis=0))
    out_ref[...] = (total[0:R] + total[R:]) * SCALE


def halo_kernel(own_ref, chip_ref, next_ref, band_ref, out_hbm, out_ref, sems):
    even = lax.axis_index("sky") % 2 == 0
    copies = []
    width = W // 4
    for c in range(4):
        cols = slice(c * width, (c + 1) * width)
        chip, following = chip_ref[:, cols].astype(F32), next_ref[:, cols].astype(F32)
        above, below = jnp.where(even, following, chip), jnp.where(even, chip, following)
        total = dot(band_ref[:, 0:2 * EDGE], jnp.concatenate([above, below], axis=0).astype(BF))
        out_ref[:, cols] = own_ref[:, cols] + (total[0:R] + total[R:]) * SCALE
        copies.append(pltpu.make_async_copy(out_ref.at[:, cols], out_hbm.at[:, cols], sems.at[c]))
        copies[-1].start()
    for copy in copies:
        copy.wait()


def vmem(n):
    return [pl.BlockSpec(memory_space=pltpu.VMEM)] * n


GRANT = 56 * 1024 * 1024
PARAMS = pltpu.CompilerParams(vmem_limit_bytes=40 * 1024 * 1024)


def tile_call(peers, *operands):
    spaces = [pltpu.SMEM, pltpu.VMEM, pltpu.SMEM, pltpu.SMEM] + [pltpu.VMEM] * 7
    return pl.pallas_call(
        tile_kernel,
        out_shape=jax.ShapeDtypeStruct((peers, MSG, LANES), BF),
        in_specs=[pl.BlockSpec(memory_space=pltpu.HBM)] * len(operands),
        out_specs=pl.BlockSpec(memory_space=pltpu.VMEM),
        scratch_shapes=[space(x.shape, x.dtype) for space, x in zip(spaces, operands)] + [
            pltpu.SemaphoreType.DMA((len(operands),)),
            pltpu.VMEM((16, 2 * LANES), F32),
            pltpu.VMEM((SPT * R, 2 * LANES), BF),
            pltpu.VMEM((R, W), F32),
            pltpu.VMEM((WINDOWS * R, 2 * LANES), BF),
            pltpu.VMEM((R, W), BF),
            pltpu.SMEM((peers,), jnp.int32),
        ],
        compiler_params=pltpu.CompilerParams(vmem_limit_bytes=GRANT),
    )(*operands)


def sum_call(received, band):
    image = jax.ShapeDtypeStruct((R, W), F32)
    rows = jax.ShapeDtypeStruct((EDGE, W), BF)
    return pl.pallas_call(
        sum_kernel,
        out_shape=(image, image, rows, rows),
        in_specs=vmem(2),
        out_specs=(pl.BlockSpec(memory_space=pltpu.HBM), *vmem(3)),
        scratch_shapes=[
            pltpu.VMEM(((SPT + 2) * R, LANES), F32),
            pltpu.VMEM((R, W), F32),
            pltpu.SemaphoreType.DMA,
        ],
        compiler_params=PARAMS,
    )(received, band)


def own_call(mid, band):
    return pl.pallas_call(
        own_kernel,
        out_shape=jax.ShapeDtypeStruct((R, W), F32),
        in_specs=vmem(2),
        out_specs=pl.BlockSpec(memory_space=pltpu.VMEM),
        compiler_params=PARAMS,
    )(mid, band)


def halo_call(own, from_chip, from_next, band):
    return pl.pallas_call(
        halo_kernel,
        out_shape=jax.ShapeDtypeStruct((R, W), F32),
        in_specs=vmem(4),
        out_specs=pl.BlockSpec(memory_space=pltpu.HBM),
        scratch_shapes=[pltpu.VMEM((R, W), F32), pltpu.SemaphoreType.DMA((4,))],
        compiler_params=PARAMS,
    )(own, from_chip, from_next, band)


def local(
    ccd_tiles, row_taps, col_taps, psf_coeffs, warp_start_x, warp_frac_x, warp_start_y, warp_frac_y,
    tile_weight, strip_owner, strip_block,
):
    peers = lax.axis_size("visit")
    operands = (
        psf_coeffs.transpose(2, 0, 1), tile_weight.reshape(1, 1), strip_owner.reshape(1, SPT), strip_block,
        ccd_tiles, row_taps, col_taps, warp_start_x, warp_frac_x, warp_start_y, warp_frac_y,
    )
    messages = tile_call(peers, *operands)
    band_across, band_own, band_halo = pl.pallas_call(
        band_kernel,
        out_shape=(
            jax.ShapeDtypeStruct((2 * LANES, 2 * LANES), BF),
            jax.ShapeDtypeStruct((2 * R, LANES), BF),
            jax.ShapeDtypeStruct((2 * R, LANES), BF),
        ),
        out_specs=tuple(vmem(3)),
        compiler_params=PARAMS,
    )()
    groups = [sorted(range(peers), key=seat)]
    received = lax.all_to_all(messages, "visit", 0, 0, tiled=True, axis_index_groups=groups)
    coadd, mid, to_chip, to_next = sum_call(received, band_across)
    size = lax.axis_size("sky")
    swap = lambda first: [p for i in range(first, size - 1, 2) for p in ((i, i + 1), (i + 1, i))]
    from_next = lax.ppermute(to_next, "sky", swap(1))
    from_chip = lax.ppermute(to_chip, "sky", swap(0))
    detection = halo_call(own_call(mid, band_own), from_chip, from_next, band_halo)
    return coadd, detection


def solution(mesh):
    tiles = ("visit", "sky")
    in_specs = (
        P(tiles, None, None),
        P(),
        P(),
        P(tiles, None, None),
        P(tiles, None),
        P(tiles, None),
        P(tiles, None),
        P(tiles, None),
        P(tiles),
        P(tiles, None, None),
        P(tiles, None),
    )
    out_specs = (P("sky", "visit"), P("sky", "visit"))
    return jax.shard_map(local, mesh=mesh, in_specs=in_specs, out_specs=out_specs, check_vma=False)
```

```python
import jax
import jax.numpy as jnp
from jax import lax
from jax.experimental import pallas as pl
from jax.experimental.pallas import tpu as pltpu
from jax.sharding import PartitionSpec as P

R = 64
W = 2048
NB = 5
KW = 41
HALO = 20
SPT = 16
SPAN = 240
WINDOWS = -(-W // SPAN)
SLOTS = 2
LANES = 128
UNIT = 16
NOTE = SLOTS * R
AUX = 24
MSG = NOTE + AUX
NOTE_LANES = 2 * UNIT
PLACE = 2 * HALO
NOTE_AT = 2 * PLACE
COUNT_AT = 3 * PLACE
EDGE = 24
NT = (((1,), (1,)), ((), ()))
BF = jnp.bfloat16
F32 = jnp.float32


def dot(left, right, dims=(((1,), (0,)), ((), ()))):
    return lax.dot_general(left, right, dims, preferred_element_type=F32)


def iota(shape, dim):
    return lax.broadcasted_iota(jnp.int32, shape, dim)


def roll(value, shift):
    width = value.shape[1]
    return pltpu.roll(value, shift % width, 1) if shift % width else value


def toeplitz(row, rows, shift=LANES - HALO):
    row = roll(row, shift % 8)
    return pltpu.roll(jnp.broadcast_to(row, (rows, row.shape[1])), shift // 8 * 8, 1, stride=1, stride_axis=0)


def sin_pi(value):
    folded = jnp.where(value > 0.5, 1.0 - value, jnp.where(value < -0.5, -1.0 - value, value))
    angle = jnp.pi * folded
    square = angle * angle
    total = jnp.full_like(angle, -1.0 / 39916800.0)
    for term in (1.0 / 362880.0, -1.0 / 5040.0, 1.0 / 120.0, -1.0 / 6.0, 1.0):
        total = total * square + term
    return total * angle


def lanczos_weights(frac):
    shape = (8, frac.shape[1])
    shift = iota(shape, 0)
    offset = jnp.broadcast_to(frac, shape) - (shift - 2).astype(F32)
    sine = sin_pi(jnp.broadcast_to(frac, shape))
    sine = jnp.where(shift % 2 == 0, sine, -sine)
    weights = 3.0 * sine * sin_pi(offset * (1.0 / 3.0)) / (jnp.pi * jnp.pi * offset * offset)
    return weights.astype(BF).astype(F32)


def seat(o):
    return (o + 2) % 8 * 4 + (o // 8 + 1) % 4


def tile_kernel(
    coeff_hbm, weight_hbm, owner_hbm, block_hbm,
    tile_hbm, row_taps_hbm, col_taps_hbm, start_x_hbm, frac_x_hbm, start_y_hbm, frac_y_hbm,
    out_ref,
    coeff_ref, weight_ref, owner_ref, block_ref,
    tile_ref, row_taps_ref, col_taps_ref, start_x_ref, frac_x_ref, start_y_ref, frac_y_ref,
    sems, taps_ref, window_ref, matched_ref, source_ref, col_ref, count_ref,
):
    pairs = [
        (row_taps_hbm, row_taps_ref), (tile_hbm, tile_ref), (col_taps_hbm, col_taps_ref),
        (coeff_hbm, coeff_ref), (frac_x_hbm, frac_x_ref), (start_x_hbm, start_x_ref),
        (start_y_hbm, start_y_ref), (frac_y_hbm, frac_y_ref), (weight_hbm, weight_ref),
        (owner_hbm, owner_ref), (block_hbm, block_ref),
    ]
    copies = [pltpu.make_async_copy(src, dst, sems.at[n]) for n, (src, dst) in enumerate(pairs)]
    for copy in copies:
        copy.start()
    taps_ref[...] = jnp.zeros_like(taps_ref)
    peers = out_ref.shape[0]
    for o in range(peers):
        count_ref[o] = 0
    out_ref[...] = jnp.zeros_like(out_ref)
    for copy in copies:
        copy.wait()
    taps_ref[0:NB, 0:KW] = row_taps_ref[...].astype(F32)
    taps_ref[8:8 + NB, 0:KW] = col_taps_ref[...].astype(F32)
    row_band = jnp.concatenate([toeplitz(taps_ref[k:k + 1, :], LANES, 0) for k in range(NB)], axis=0).astype(BF)
    col_bands = [toeplitz(taps_ref[8 + k:9 + k, 0:LANES], R)[:, 0:R].astype(BF) for k in range(NB)]
    empty = jnp.zeros((R, R), BF)
    moved = roll(tile_ref[0].astype(F32), HALO)
    before = iota((R, LANES), 1) < HALO
    for s in range(SPT + 1):
        strip = moved[:, s % SPT * LANES:(s % SPT + 1) * LANES]
        if s % SPT == 0:
            strip = jnp.where(before == (s > 0), strip, 0.0)
        strip = strip.astype(BF)
        if s < SPT:
            window_ref[s * R:(s + 1) * R, 0:LANES] = strip
        if s > 0:
            window_ref[(s - 1) * R:s * R, LANES:] = strip
    group = 16
    width = group * LANES
    for g in range(SPT // group):
        rows = group * R
        window = window_ref[g * rows:(g + 1) * rows, :]
        across = dot(window, row_band, NT).astype(BF)
        column = iota((1, width), 1) + g * width
        x_coord = (2 * column - (W - 1)).astype(F32) / (W - 1)
        y_coord = (2 * iota((R, 1), 0) - (R - 1)).astype(F32) / (R - 1)
        terms = [
            jnp.concatenate(
                [across[j * R:(j + 1) * R, k * LANES:(k + 1) * LANES] for j in range(group)], axis=1
            )
            for k in range(NB)
        ]
        basis_terms = []
        for first in range(0, NB, 4):
            count = min(4, NB - first)
            bands = [
                jnp.concatenate([col_bands[first + k] if k == j else empty for j in range(count)], axis=1)
                for k in range(count)
            ]
            found = dot(jnp.concatenate(bands, axis=0), jnp.concatenate(terms[first:first + count], axis=0))
            basis_terms += [found[k * R:(k + 1) * R] for k in range(count)]
        matched = jnp.zeros((R, width), F32)
        for k in range(NB):
            coeff_map = coeff_ref[0, 0, k] + coeff_ref[1, 0, k] * x_coord + coeff_ref[2, 0, k] * y_coord
            matched = matched + coeff_map * basis_terms[k]
        matched_ref[:, g * width:(g + 1) * width] = matched.astype(BF).astype(F32)
    for n in range(WINDOWS):
        first = n * SPAN - 2
        blocks = [(first // LANES + j) % SPT * LANES for j in range(3)]
        region = jnp.concatenate([matched_ref[:, at:at + LANES] for at in blocks], axis=1)
        source_ref[n * R:(n + 1) * R, :] = roll(region, -(first % LANES))[:, 0:2 * LANES].astype(BF)
    weights_x = lanczos_weights(frac_x_ref[...])
    chunk = 1024
    order = iota((2 * LANES, chunk), 0).astype(F32).astype(BF)
    for c in range(W // chunk):
        cols = slice(c * chunk, (c + 1) * chunk)
        start = start_x_ref[:, cols]
        place = ((start.astype(F32) + 0.5) * (1.0 / SPAN)).astype(jnp.int32)
        tap = order - (start - place * SPAN).astype(F32).astype(BF)
        taps = jnp.zeros((2 * LANES, chunk), BF)
        for s in range(6):
            taps = jnp.where(tap == s, weights_x[s:s + 1, cols].astype(BF), taps)
        found = dot(source_ref[...], taps)
        place = jnp.broadcast_to(place, (8, chunk))
        total = found[0:R].reshape(R // 8, 8, chunk)
        for s in range(1, WINDOWS):
            part = found[s * R:(s + 1) * R].reshape(R // 8, 8, chunk)
            total = jnp.where((place == s)[None], part, total)
        col_ref[:, cols] = total.reshape(R, chunk).astype(BF)
    weights_y = lanczos_weights(frac_y_ref[...])
    step = iota((R, R), 0) - start_y_ref[...]
    warp_y = jnp.zeros((R, R), F32)
    for s in range(6):
        warp_y = jnp.where(step == s - 2, weights_y[s:s + 1, :], warp_y)
    warped = dot(warp_y.T.astype(BF), col_ref[...]).astype(BF)
    weight = weight_ref[...].astype(F32)
    row = iota((AUX, LANES), 0)
    lane = iota((AUX, LANES), 1)
    place = lane - NOTE_AT
    last = row - (AUX - 8)
    noted = (last >= 0) & (place >= 0) & (place < NOTE_LANES)
    base = jnp.where(noted & (last == 2), weight, 0.0).astype(BF)
    for o in range(peers):
        out_ref[o, NOTE:MSG, :] = base

    def add(owner, piece):
        owner = seat(owner)
        out_ref[owner, NOTE:MSG, :] = (out_ref[owner, NOTE:MSG, :].astype(F32) + piece).astype(BF)

    def add_edges(owner, strip, lanes, side):
        strip = strip.astype(F32)
        units = []
        for t in range(AUX // 8):
            at = lane[0:8] - side * HALO
            unit = jnp.where(lane[0:8] == COUNT_AT + side, 1.0, 0.0)
            for f in range(3):
                n = 3 * t + f
                if n < R // 8:
                    part = roll(strip[n * 8:(n + 1) * 8], f * PLACE + side * HALO - lanes)
                    unit = jnp.where((at >= f * PLACE) & (at < f * PLACE + HALO), part, unit)
            units.append(unit)
        add(owner, jnp.concatenate(units, axis=0))

    for s in range(SPT):
        owner, block = owner_ref[0, s], block_ref[0, s]
        slot = count_ref[owner]
        count_ref[owner] = slot + 1
        strip = warped[:, s * LANES:(s + 1) * LANES]
        out_ref[seat(owner), pl.ds(pl.multiple_of(slot * R, R), R), :] = strip
        note = jnp.where(last == 0, weight, jnp.where(last == 1, block.astype(F32), 0.0))
        add(owner, jnp.where(noted & (place // UNIT == slot), note, 0.0))

        @pl.when((block == SPT - 1) | (block == 0))
        def _():
            pl.when((block > 0) & (owner < peers - 1))(
                lambda: add_edges(owner + 1, strip, LANES - HALO, 0)
            )
            pl.when((block == 0) & (owner > 0))(lambda: add_edges(owner - 1, strip, 0, 1))


def split(value):
    high = value.astype(BF)
    return high, (value - high.astype(F32)).astype(BF)


def taper_bands(width, rows, shift):
    lane = iota((1, width), 1)
    at = lane - HALO
    taps = jnp.where(lane < KW, 441 - at * at, 0).astype(F32)
    high, low = split(toeplitz(taps, rows, shift))
    return jnp.concatenate([high, low], axis=0)


def band_kernel(across_ref, down_ref):
    across_ref[...] = taper_bands(2 * LANES, LANES, 0)
    down_ref[...] = taper_bands(LANES, R, EDGE - HALO)


def sum_kernel(in_ref, band_ref, coadd_ref, mid_ref, chip_ref, next_ref, stack_ref):
    peers = in_ref.shape[0]
    depth = peers * NOTE_LANES
    aux = [in_ref[v, NOTE:MSG, :].astype(F32) for v in range(peers)]
    notes = []
    per_row = LANES // NOTE_LANES
    lane = iota((8, LANES), 1)
    for q in range(peers // per_row):
        total = jnp.zeros((8, LANES), F32)
        for j in range(per_row):
            note = roll(aux[q * per_row + j][AUX - 8:], j * NOTE_LANES - NOTE_AT)
            total = jnp.where(lane // NOTE_LANES == j, note, total)
        notes.append(total)
    notes = jnp.concatenate(notes, axis=1)
    weight, block, peer_weight = notes[0:1], notes[1:2], notes[2:3]
    same = iota((UNIT, depth), 0) == iota((UNIT, depth), 1) % UNIT
    spread = jnp.concatenate(
        [jnp.where(same, jnp.where(block == b, weight, 0.0), 0.0) for b in range(SPT)], axis=0
    ).astype(BF)
    parts = []
    for g in range(R // UNIT):
        pieces = [
            in_ref[v, slot * R + g * UNIT:slot * R + (g + 1) * UNIT, :]
            for v in range(peers) for slot in range(SLOTS)
        ]
        parts.append(jnp.concatenate(pieces, axis=0))
    parts.append(jnp.ones((depth, LANES), BF))
    total = dot(spread, jnp.concatenate(parts, axis=1))
    scale = 1.0 / (total[:, R // UNIT * LANES:] + 1.0)
    for b in range(SPT):
        for g in range(R // UNIT):
            rows = slice(b * UNIT, (b + 1) * UNIT)
            value = total[rows, g * LANES:(g + 1) * LANES] * scale[rows]
            coadd_ref[g * UNIT:(g + 1) * UNIT, b * LANES:(b + 1) * LANES] = value
            stack_ref[(b + 1) * R + g * UNIT:(b + 1) * R + (g + 1) * UNIT, :] = value
    same = iota((AUX, depth), 0) == iota((AUX, depth), 1) % NOTE_LANES
    gap = jnp.zeros((NOTE_LANES - AUX, LANES), F32)
    edges = jnp.concatenate([x for v in range(peers) for x in (aux[v], gap)], axis=0).astype(BF)
    edges = dot(jnp.where(same, peer_weight, 0.0).astype(BF), edges)
    for side, block in enumerate((0, SPT + 1)):
        sum_weight = edges[AUX - 8:AUX - 7, COUNT_AT + side:COUNT_AT + side + 1]
        value = edges * (1.0 / (sum_weight + 1.0))
        for n in range(R // 8):
            t, f = n // 3, n % 3
            to = (LANES - HALO, 0)[side] - f * PLACE - side * HALO
            stack_ref[block * R + n * 8:block * R + n * 8 + 8, :] = roll(value[t * 8:t * 8 + 8], to)
    band = band_ref[...]
    moved = roll(stack_ref[...], HALO)
    strips = (SPT + 1) * R
    moved = jnp.where(iota((strips, LANES), 1) < HALO, moved[0:strips], moved[R:])
    window = jnp.concatenate(
        [jnp.concatenate([part[0:SPT * R], part[R:]], axis=1) for part in split(moved)], axis=0
    )
    mid = dot(window, band, NT)
    mid = (mid[0:SPT * R] + mid[SPT * R:])
    mid = mid[:, 0:LANES] + mid[:, LANES:]
    for s in range(SPT):
        mid_ref[:, s * LANES:(s + 1) * LANES] = mid[s * R:(s + 1) * R]
    even = lax.axis_index("sky") % 2 == 0
    first, last = mid_ref[0:EDGE, :], mid_ref[R - EDGE:R, :]
    chip_ref[...] = jnp.where(even, last, first).astype(BF)
    next_ref[...] = jnp.where(even, first, last).astype(BF)


def down_kernel(mid_ref, chip_ref, next_ref, band_ref, out_ref):
    norm = sum((1.0 - (a / 21.0) ** 2) ** 2 for a in range(-HALO, HALO + 1))
    even = lax.axis_index("sky") % 2 == 0
    chip, following = chip_ref[...].astype(F32), next_ref[...].astype(F32)
    above, below = jnp.where(even, following, chip), jnp.where(even, chip, following)
    rows = jnp.concatenate([above, mid_ref[...], below], axis=0)
    band = band_ref[:, 0:R + 2 * EDGE]
    high, low = split(rows)
    total = dot(jnp.concatenate([band, band], axis=1), jnp.concatenate([high, low], axis=0))
    out_ref[...] = (total[0:R] + total[R:]) * (1.0 / (441.0 * 441.0 * norm))


def vmem(n):
    return [pl.BlockSpec(memory_space=pltpu.VMEM)] * n


GRANT = 56 * 1024 * 1024
PARAMS = pltpu.CompilerParams(vmem_limit_bytes=40 * 1024 * 1024)


def tile_call(peers, *operands):
    spaces = [pltpu.SMEM, pltpu.VMEM, pltpu.SMEM, pltpu.SMEM] + [pltpu.VMEM] * 7
    return pl.pallas_call(
        tile_kernel,
        out_shape=jax.ShapeDtypeStruct((peers, MSG, LANES), BF),
        in_specs=[pl.BlockSpec(memory_space=pltpu.HBM)] * len(operands),
        out_specs=pl.BlockSpec(memory_space=pltpu.VMEM),
        scratch_shapes=[space(x.shape, x.dtype) for space, x in zip(spaces, operands)] + [
            pltpu.SemaphoreType.DMA((len(operands),)),
            pltpu.VMEM((16, 2 * LANES), F32),
            pltpu.VMEM((SPT * R, 2 * LANES), BF),
            pltpu.VMEM((R, W), F32),
            pltpu.VMEM((WINDOWS * R, 2 * LANES), BF),
            pltpu.VMEM((R, W), BF),
            pltpu.SMEM((peers,), jnp.int32),
        ],
        compiler_params=pltpu.CompilerParams(vmem_limit_bytes=GRANT),
    )(*operands)


def sum_call(received, band):
    image = jax.ShapeDtypeStruct((R, W), F32)
    rows = jax.ShapeDtypeStruct((EDGE, W), BF)
    return pl.pallas_call(
        sum_kernel,
        out_shape=(image, image, rows, rows),
        in_specs=vmem(2),
        out_specs=tuple(vmem(4)),
        scratch_shapes=[pltpu.VMEM(((SPT + 2) * R, LANES), F32)],
        compiler_params=PARAMS,
    )(received, band)


def down_call(mid, from_chip, from_next, band):
    return pl.pallas_call(
        down_kernel,
        out_shape=jax.ShapeDtypeStruct((R, W), F32),
        in_specs=vmem(4),
        out_specs=pl.BlockSpec(memory_space=pltpu.VMEM),
        compiler_params=PARAMS,
    )(mid, from_chip, from_next, band)


def local(
    ccd_tiles, row_taps, col_taps, psf_coeffs, warp_start_x, warp_frac_x, warp_start_y, warp_frac_y,
    tile_weight, strip_owner, strip_block,
):
    peers = lax.axis_size("visit")
    operands = (
        psf_coeffs.transpose(2, 0, 1), tile_weight.reshape(1, 1), strip_owner.reshape(1, SPT), strip_block,
        ccd_tiles, row_taps, col_taps, warp_start_x, warp_frac_x, warp_start_y, warp_frac_y,
    )
    messages = tile_call(peers, *operands)
    band_across, band_down = pl.pallas_call(
        band_kernel,
        out_shape=(jax.ShapeDtypeStruct((2 * LANES, 2 * LANES), BF), jax.ShapeDtypeStruct((2 * R, LANES), BF)),
        out_specs=tuple(vmem(2)),
        compiler_params=PARAMS,
    )()
    groups = [sorted(range(peers), key=seat)]
    received = lax.all_to_all(messages, "visit", 0, 0, tiled=True, axis_index_groups=groups)
    coadd, mid, to_chip, to_next = sum_call(received, band_across)
    size = lax.axis_size("sky")
    swap = lambda first: [p for i in range(first, size - 1, 2) for p in ((i, i + 1), (i + 1, i))]
    from_next = lax.ppermute(to_next, "sky", swap(1))
    from_chip = lax.ppermute(to_chip, "sky", swap(0))
    detection = down_call(mid, from_chip, from_next, band_down)
    return coadd, detection


def solution(mesh):
    tiles = ("visit", "sky")
    in_specs = (
        P(tiles, None, None),
        P(),
        P(),
        P(tiles, None, None),
        P(tiles, None),
        P(tiles, None),
        P(tiles, None),
        P(tiles, None),
        P(tiles),
        P(tiles, None, None),
        P(tiles, None),
    )
    out_specs = (P("sky", "visit"), P("sky", "visit"))
    return jax.shard_map(local, mesh=mesh, in_specs=in_specs, out_specs=out_specs, check_vma=False)
```
